512 devices in a mesh: view: 4 (over x_hi, core), brick: 128 (over z, y, x_lo).
Axes of the slice: x: 4 (x_hi: 2, x_lo: 2; x = x_hi * 2 + x_lo), y: 4, z: 16, core: 2. Of those that a mesh axis runs over, the one named last changes fastest.
Arguments:
- estimate: float32 [128, 2048, 128], P('brick'), may hold values from 0.5 to 2
- observed: float32 [4, 128, 2048, 128], P('view', None, 'brick'), may hold values from 0.25 to 4
- long_taps: float32 [4, 31], P('view'), may hold values from 0.05 to 1
- short_taps: float32 [4, 2, 7], P('view'), may hold values from 0.05 to 1
- brick_map: int32 [4, 128], P('view'), may hold values from 0 to 127, each once within a row
- valid_rows: int32 [4, 128], P('view'), may hold values from 512 to 2048
Outputs:
- refined: float32 [128, 2048, 128], P('brick')
The draws below stay inside these ranges and needn't reach their ends.
Inputs may be any that keep to these rules, and one draw needn't show every extreme that they name: Each view's row of brick_map names every reference brick exactly once.
All inputs are finite; a program needn't handle non-finite values.
Results may differ from the reference program's by a relative error of at most 0.0001.
Values sent between devices are 32-bit elements; how exact they have to be, the bound alone decides.
A program may use at most 64 MiB of HBM per device.

```python
import math
import jax
import jax.numpy as jnp
from jax import lax

TZ = 1
X = 128
TAPS_LONG = 31
TAPS_SHORT = 7
ITERS = 2
VIEWS = 4
BRICKS = 128
Z = 128
Y = 2048


def with_ends(entries, own_key, smallest, largest):
    index_at = [jax.random.randint(jax.random.fold_in(own_key, axis), (), 0, length) for axis, length in enumerate(entries.shape)]
    widest = entries.shape.index(max(entries.shape))
    next_to = index_at[:widest] + [(index_at[widest] + 1) % entries.shape[widest]] + index_at[widest + 1:]
    return entries.at[tuple(index_at)].set(smallest).at[tuple(next_to)].set(largest)


def steps_of(stream_key, extent, shards, low, largest):
    gain = 1.0
    for dim, shards_of in shards:
        draws = jax.random.uniform(jax.random.fold_in(jax.random.fold_in(stream_key, 6), dim), (shards_of,), jnp.float32, low / len(shards), largest / len(shards))
        gain = gain * jnp.repeat(jnp.exp(draws), extent[dim] // shards_of).reshape((-1,) + (1,) * (len(extent) - 1 - dim))
    return gain


def setup_inputs(seed: int = 0) -> dict:
    keys = jax.random.split(jax.random.key(seed), 7)
    estimate = jnp.clip(jnp.exp(math.log(2.0) - 1.3862944 * jax.random.uniform(keys[0], (Z, Y, X), jnp.float32) ** steps_of(keys[0], (Z, Y, X), ((0, 128),), -0.2, 0.2)), 0.5, 2.0)
    observed = jnp.clip(jnp.exp(math.log(4.0) - 2.7725887 * jax.random.uniform(keys[1], (VIEWS, Z, Y, X), jnp.float32) ** steps_of(keys[1], (VIEWS, Z, Y, X), ((0, 4), (2, 128)), -0.2, 0.2)), 0.25, 4.0)
    long_taps = jnp.clip(jnp.exp(math.log(1.0) - 2.9957323 * jax.random.uniform(keys[2], (VIEWS, TAPS_LONG), jnp.float32) ** steps_of(keys[2], (VIEWS, TAPS_LONG), ((0, 4),), -0.2, 0.2)), 0.05, 1.0)
    short_taps = jnp.clip(jnp.exp(math.log(1.0) - 2.9957323 * jax.random.uniform(keys[3], (VIEWS, 2, TAPS_SHORT), jnp.float32) ** steps_of(keys[3], (VIEWS, 2, TAPS_SHORT), ((0, 4),), -0.2, 0.2)), 0.05, 1.0)
    brick_map = jax.vmap(lambda own: jax.random.permutation(own, BRICKS))(jax.random.split(keys[4], VIEWS)).reshape((VIEWS, BRICKS)).astype(jnp.int32)
    valid_rows = with_ends(jax.random.randint(keys[5], (VIEWS, BRICKS), Y // 4, Y + 1), jax.random.fold_in(keys[5], 1), Y // 4, Y).astype(jnp.int32)
    return dict(estimate=estimate, observed=observed, long_taps=long_taps, short_taps=short_taps, brick_map=brick_map, valid_rows=valid_rows)


def normalized(kernel):
    return kernel / jnp.sum(kernel)


def blur_axis(volume, kernel, dimension, adjoint):
    kernel_size = kernel.shape[0]
    radius = kernel_size // 2
    if adjoint:
        kernel = kernel[::-1]
    padding = [(0, 0)] * 3
    padding[dimension] = (radius, radius)
    padded = jnp.pad(volume, padding)
    length = volume.shape[dimension]
    summed = jnp.zeros(volume.shape, jnp.float32)
    for offset in range(kernel_size):
        summed = summed + kernel[offset] * lax.slice_in_dim(padded, offset, offset + length, axis=dimension)
    return summed


def relay(volume, brick_order):
    bricks = volume.reshape(BRICKS, TZ, volume.shape[1], volume.shape[2])
    return bricks[brick_order].reshape(volume.shape)


def reference(estimate, observed, long_taps, short_taps, brick_map, valid_rows):
    current = estimate
    row_ids = jnp.arange(Y, dtype=jnp.int32)
    for iteration in range(ITERS):
        log_total = jnp.zeros(current.shape, jnp.float32)
        for view_index in range(VIEWS):
            kernel_long = normalized(long_taps[view_index])
            kernel_plane = normalized(short_taps[view_index, 0])
            kernel_column = normalized(short_taps[view_index, 1])
            forward_map = brick_map[view_index].astype(jnp.int32)
            inverse = jnp.argsort(forward_map).astype(jnp.int32)
            framed = relay(current, forward_map)
            blurred = blur_axis(framed, kernel_long, 1, False)
            blurred = blur_axis(blurred, kernel_plane, 0, False)
            blurred = blur_axis(blurred, kernel_column, 2, False)
            limits = jnp.repeat(valid_rows[view_index], TZ)
            valid_mask = (row_ids[None, :] < limits[:, None])[:, :, None]
            ratios = jnp.where(valid_mask, observed[view_index] / blurred, 1.0)
            spread_back = blur_axis(ratios, kernel_plane, 0, True)
            spread_back = blur_axis(spread_back, kernel_column, 2, True)
            spread_back = blur_axis(spread_back, kernel_long, 1, True)
            log_total = log_total + jnp.log(relay(spread_back, inverse))
        current = current * jnp.exp(log_total)
    return current
```

```python
import jax
import jax.numpy as jnp
from jax import lax
from jax.experimental import pallas as pl
from jax.experimental.pallas import tpu as pltpu
from jax.sharding import Mesh
from jax.sharding import PartitionSpec as P

F32, BF16 = jnp.float32, jnp.bfloat16
ITERS = 2
VIEWS, BRICKS, ROWS, COLS = 4, 128, 2048, 128
NZ, NY = 16, 4
BLOCK = 128
OWN = 4
WIDE = OWN + 6
HALO = 16
TALL = BLOCK + 2 * HALO
AXES = ("xh", "core", "z", "y", "xl")
MESH = pl.DeviceIdType.MESH


def split(x):
    head = x.astype(BF16)
    return head, (x - head.astype(F32)).astype(BF16)


def dot3(ah, al, bh, bl):
    def dot(a, b):
        return jnp.dot(a, b, preferred_element_type=F32)

    return dot(ah, bh) + (dot(al, bh) + dot(ah, bl))


def exchange_halves(a, b):
    axis = a.ndim - 2
    top = lax.broadcasted_iota(jnp.int32, a.shape, axis) < 4
    first = jnp.where(top, a, pltpu.roll(b, 4, axis))
    second = jnp.where(top, pltpu.roll(a, 4, axis), b)
    return first, second


def loop(n, body):
    def step(i, carry):
        body(i)
        return carry

    lax.fori_loop(0, n, step, 0)


def kernel(
    est, obs, long_taps, short_taps, brick_map, valid_rows, out,
    par, turned, s1, r1, s2, r2, obs_out, obs_in, ext, rows_done, spread, tall, corr,
    x2, r3, s4, gathered, tile_taps, bf_h, bf_l, bb_h, bb_l, tf_h, tf_l, tb_h, tb_l,
    par_s, par_r, z_s, z_r, obs_s, obs_r, p_s, p_r, ec_s, ec_r, er_s, er_r, uc_s, uc_r, ur_s, ur_r,
    q_s, q_r, y_s, y_r, v_s, v_r,
):
    xh, core, z, y, xl = (lax.axis_index(a) for a in AXES)
    x = 2 * xh + xl
    kk = 4 * xl + lax.rem(y + x, NY)
    k = 8 * xh + kk
    g = 2 * k + core
    view = 2 * xh + core
    slab = 2 * y + xl
    place = view * 8 + slab

    def at_kk(xh_, core_, kk_):
        xl_ = kk_ // 4
        return xh_, core_, z, lax.rem(lax.rem(kk_, 4) + 8 - 2 * xh_ - xl_, NY), xl_

    def slab_of(kk_):
        _, _, _, y_, xl_ = at_kk(xh, core, kk_)
        return 2 * y_ + xl_

    def at_g(g_):
        k_ = g_ // 2
        return at_kk(k_ // 8, lax.rem(g_, 2), lax.rem(k_, 8))

    def at_z(z_):
        return xh, core, z_, y, xl

    def at_place(place_):
        return place_ // 16, lax.rem(place_ // 8, 2), z, lax.rem(place_ // 2, 4), lax.rem(place_, 2)

    def at_view(view_):
        return view_ // 2, lax.rem(view_, 2), z, y, xl

    def g_of(place_):
        xh_, _, _, y_, xl_ = at_place(place_)
        x_ = 2 * xh_ + xl_
        return 2 * (4 * x_ + lax.rem(y_ + x_, NY)) + lax.rem(place_ // 8, 2)

    def remote(src, dst, send, recv, device):
        return pltpu.make_async_remote_copy(
            src_ref=src, dst_ref=dst, send_sem=send, recv_sem=recv, device_id=device, device_id_type=MESH
        )

    left, right = lax.rem(g + 31, 32), lax.rem(g + 1, 32)
    above, below = lax.rem(z + NZ - 1, NZ), lax.rem(z + 1, NZ)

    barrier = pltpu.get_barrier_semaphore()

    @pl.loop(1, NZ)
    def _(d):
        pl.semaphore_signal(barrier, inc=1, device_id=at_z(lax.rem(z + d, NZ)), device_id_type=MESH)

    @pl.loop(1, 32)
    def _(n):
        pl.semaphore_signal(barrier, inc=1, device_id=at_place(lax.rem(place + n, 32)), device_id_type=MESH)

    par[view] = jnp.zeros((8, 128), F32)
    par[view, 0:1, :] = brick_map[...].astype(F32)
    par[view, 1:2, :] = valid_rows[...].astype(F32)
    par[view, 2:3, 0:31] = long_taps[...]
    par[view, 3:5, 0:7] = short_taps[...]

    pl.semaphore_wait(barrier, NZ - 1 + 31)

    def par_copy(m, source, device):
        return remote(par.at[source], par.at[source], par_s.at[m], par_r.at[m], device)

    for m in range(1, VIEWS):
        par_copy(m, view, at_view(lax.rem(view + m, VIEWS))).start()

    def piece_for(zt):
        block = est[pl.ds(pl.multiple_of(BLOCK * zt, BLOCK), BLOCK), :]
        turned[...] = block.T
        half = turned[pl.ds(pl.multiple_of(64 * xh, 64), 64), :].reshape(4, 2, 8, 128)
        first, second = exchange_halves(half[:, 0], half[:, 1])
        return jnp.where(core == 0, first, second)

    def z_copy(d, source, device):
        return remote(s1.at[d], r1.at[source], z_s.at[d], z_r.at[d], device)

    def far_first(i):
        return 8 + ((i + 1) // 2) * (1 - 2 * lax.rem(i, 2))

    @pl.loop(0, NZ - 1)
    def _(i):
        d = far_first(i)
        zt = lax.rem(z + d, NZ)
        s1[d] = piece_for(zt)
        z_copy(d, z, at_z(zt)).start()

    r1[z] = piece_for(z)

    @pl.loop(0, 16)
    def _(r):
        obs_out[pl.ds(r, 128, stride=16), :] = obs[pl.ds(r, 128, stride=16), :].T

    def obs_copy(n, g_, view_, slab_, device):
        src = obs_out.at[pl.ds(pl.multiple_of(64 * g_, 64), 64)]
        return remote(src, obs_in.at[view_, slab_], obs_s.at[n], obs_r.at[n], device)

    @pl.loop(1, 32)
    def _(n):
        to = lax.rem(place + n, 32)
        obs_copy(n, g_of(to), view, slab, at_place(to)).start()

    obs_in[view, slab] = obs_out[pl.ds(pl.multiple_of(64 * g, 64), 64), :]

    for m in range(1, VIEWS):
        par_copy(m, lax.rem(view + VIEWS - m, VIEWS), at_view(lax.rem(view + m, VIEWS))).wait_recv()
    lane = lax.broadcasted_iota(jnp.int32, (1, 128), 1)
    order = lax.broadcasted_iota(jnp.int32, (128, 128), 0)
    brick = (lax.rem(order, 16) * 8 + order // 16).astype(F32)
    tall_lane = lax.broadcasted_iota(jnp.int32, (BLOCK, TALL), 1)
    inside = jnp.logical_and(
        jnp.logical_or(tall_lane >= HALO, z > 0), jnp.logical_or(tall_lane < HALO + BLOCK, z < NZ - 1)
    )
    for v in range(VIEWS):
        bricks, long_row, plane, column = (par[v, i : i + 1, :] for i in (0, 2, 3, 4))
        long_row, plane, column = (t / jnp.sum(t, axis=1, keepdims=True) for t in (long_row, plane, column))
        matrix = jnp.zeros((128, 128), F32)
        for t in range(7):
            near = pltpu.roll(bricks, (3 - t) % 128, 1)
            near = jnp.where(jnp.logical_and(lane + (t - 3) >= 0, lane + (t - 3) < BRICKS), near, -1.0)
            matrix += jnp.where(brick == near, plane[:, t : t + 1], 0.0)
            tile_taps[8 * v + t : 8 * v + t + 1, :] = jnp.broadcast_to(column[:, t : t + 1], (1, 128))
        bf_h[v], bf_l[v] = split(matrix)
        bb_h[v], bb_l[v] = split(matrix.T)
        padded = jnp.concatenate([long_row, jnp.zeros((1, 128), F32)], axis=1)
        wide = jnp.broadcast_to(padded, (BLOCK, 256))
        toeplitz = pltpu.roll(wide, 1, 1, stride=1, stride_axis=0)[:, :TALL]
        tf_h[pl.ds(BLOCK * v, BLOCK), :], tf_l[pl.ds(BLOCK * v, BLOCK), :] = split(
            jnp.where(inside, toeplitz, 0.0)
        )
        high = jnp.broadcast_to(padded, (256, 256))
        flipped = pltpu.roll(high, 225, 1, stride=1, stride_axis=0)[:, :128].T[:, :TALL]
        tb_h[pl.ds(BLOCK * v, BLOCK), :], tb_l[pl.ds(BLOCK * v, BLOCK), :] = split(
            jnp.where(inside, flipped, 0.0)
        )

    @pl.loop(0, NZ - 1)
    def _(i):
        d = far_first(i)
        z_copy(d, lax.rem(z + NZ - d, NZ), at_z(lax.rem(z + d, NZ))).wait_recv()

    @pl.loop(0, 8)
    def _(m):
        first, second = exchange_halves(r1[2 * m], r1[2 * m + 1])
        for i in range(4):
            s2[pl.ds(pl.multiple_of(64 * (2 * i) + 8 * m, 8), 8), :] = first[i]
            s2[pl.ds(pl.multiple_of(64 * (2 * i + 1) + 8 * m, 8), 8), :] = second[i]

    def p_copy(n, kt, source):
        src = s2.at[pl.ds(pl.multiple_of(64 * kt, 64), 64)]
        dst = r2.at[pl.ds(pl.multiple_of(64 * slab_of(source), 64), 64)]
        return remote(src, dst, p_s.at[n], p_r.at[n], at_kk(xh, core, kt))

    @pl.loop(1, 8)
    def _(n):
        p_copy(n, lax.rem(kk + n, 8), kk).start()

    mine = pl.ds(pl.multiple_of(64 * slab, 64), 64)
    r2[mine, :] = s2[pl.ds(pl.multiple_of(64 * kk, 64), 64), :]

    @pl.loop(1, 8)
    def _(n):
        p_copy(n, lax.rem(kk + n, 8), lax.rem(kk + 8 - n, 8)).wait_recv()

    for c in range(OWN):
        ext[0, 3 + c, HALO : HALO + BLOCK, :] = r2[pl.ds(c, 128, stride=4), :].T

    @pl.loop(1, 32)
    def _(n):
        source = lax.rem(place + 32 - n, 32)
        to = lax.rem(place + n, 32)
        obs_copy(n, g_of(to), source // 8, lax.rem(source, 8), at_place(to)).wait_recv()

    middle = pl.ds(HALO, BLOCK)

    def ext_columns(it):
        return (
            remote(ext.at[it, 3:6, middle], ext.at[it, 7:10, middle], ec_s.at[it, 0], ec_r.at[it, 0], at_g(left)),
            remote(ext.at[it, 4:7, middle], ext.at[it, 0:3, middle], ec_s.at[it, 1], ec_r.at[it, 1], at_g(right)),
        )

    def ext_rows(it):
        first, last = pl.ds(HALO, HALO), pl.ds(BLOCK, HALO)
        return (
            remote(ext.at[it, :, first], ext.at[it, :, pl.ds(HALO + BLOCK, HALO)], er_s.at[it, 0], er_r.at[it, 0], at_z(above)),
            remote(ext.at[it, :, last], ext.at[it, :, pl.ds(0, HALO)], er_s.at[it, 1], er_r.at[it, 1], at_z(below)),
        )

    def spread_columns(it, v):
        return (
            remote(spread.at[it, v, 3:6], spread.at[it, v, 7:10], uc_s.at[it, v, 0], uc_r.at[it, v, 0], at_g(left)),
            remote(spread.at[it, v, 4:7], spread.at[it, v, 0:3], uc_s.at[it, v, 1], uc_r.at[it, v, 1], at_g(right)),
        )

    def tall_rows(it, v):
        first, last = pl.ds(HALO, HALO), pl.ds(BLOCK, HALO)
        return (
            remote(tall.at[it, v, :, first], tall.at[it, v, :, pl.ds(HALO + BLOCK, HALO)], ur_s.at[it, v, 0], ur_r.at[it, v, 0], at_z(above)),
            remote(tall.at[it, v, :, last], tall.at[it, v, :, pl.ds(0, HALO)], ur_s.at[it, v, 1], ur_r.at[it, v, 1], at_z(below)),
        )

    def column_inside(i):
        at = OWN * g + i - 3
        return jnp.logical_and(at >= 0, at < COLS)

    row_ids = (BLOCK * z + lax.broadcasted_iota(jnp.int32, (BLOCK, 128), 0)).astype(F32)

    for it in range(ITERS):
        for copy in ext_columns(it):
            copy.start()
        for copy in ext_columns(it):
            copy.wait_recv()
        for copy in ext_rows(it):
            copy.start()
        for copy in ext_rows(it):
            copy.wait_recv()

        @pl.loop(0, WIDE)
        def _(i):
            head, tail = split(jnp.where(column_inside(i), ext[it, i], 0.0))
            rows_done[i] = dot3(tf_h[...], tf_l[...], head, tail)

        @pl.loop(0, VIEWS)
        def _(v):
            part = pl.ds(pl.multiple_of(BLOCK * v, BLOCK), BLOCK)

            @pl.loop(0, OWN)
            def _(c):
                blurred = jnp.zeros((BLOCK, 128), F32)
                for t in range(7):
                    blurred += tile_taps[pl.ds(8 * v + t, 1), :] * rows_done[c + t, part, :]
                blurred = dot3(*split(blurred), bf_h[v], bf_l[v])
                seen = obs_in[v, :, pl.ds(pl.multiple_of(16 * c, 16), 16), :].reshape(BLOCK, 128)
                ratio = jnp.where(row_ids < par[v, 1:2, :], seen / blurred, 1.0)
                spread[it, v, 3 + c] = dot3(*split(ratio), bb_h[v], bb_l[v])

            for copy in spread_columns(it, v):
                copy.start()

        @pl.loop(0, VIEWS)
        def _(v):
            for copy in spread_columns(it, v):
                copy.wait_recv()

            @pl.loop(0, OWN)
            def _(c):
                total = jnp.zeros((BLOCK, 128), F32)
                for t in range(7):
                    tap = jnp.where(column_inside(c + t), tile_taps[pl.ds(8 * v + 6 - t, 1), :], 0.0)
                    total += tap * spread[it, v, c + t]
                tall[it, v, c, HALO : HALO + BLOCK, :] = total

            for copy in tall_rows(it, v):
                copy.start()

        @pl.loop(0, VIEWS)
        def _(v):
            for copy in tall_rows(it, v):
                copy.wait_recv()
            part = pl.ds(pl.multiple_of(BLOCK * v, BLOCK), BLOCK)

            @pl.loop(0, OWN)
            def _(c):
                corr[v, c] = dot3(tb_h[part, :], tb_l[part, :], *split(tall[it, v, c]))

        for c in range(OWN):
            log_total = jnp.log(corr[0, c] * corr[1, c]) + jnp.log(corr[2, c] * corr[3, c])
            current = ext[it, 3 + c, HALO : HALO + BLOCK, :] * jnp.exp(log_total)
            if it < ITERS - 1:
                ext[it + 1, 3 + c, HALO : HALO + BLOCK, :] = current
            else:
                x2[pl.ds(c, 128, stride=4), :] = current.T

    def q_copy(n, kt, source):
        src = x2.at[pl.ds(pl.multiple_of(64 * slab_of(kt), 64), 64)]
        return remote(src, r3.at[source], q_s.at[n], q_r.at[n], at_kk(xh, core, kt))

    @pl.loop(1, 8)
    def _(n):
        q_copy(n, lax.rem(kk + n, 8), kk).start()

    r3[kk] = x2[mine, :]

    @pl.loop(1, 8)
    def _(n):
        q_copy(n, lax.rem(kk + n, 8), lax.rem(kk + 8 - n, 8)).wait_recv()

    @pl.loop(0, 8)
    def _(m):
        part = pl.ds(pl.multiple_of(8 * m, 8), 8)
        for i in range(4):
            first, second = exchange_halves(r3[2 * i, part, :], r3[2 * i + 1, part, :])
            s4[2 * m, i] = first
            s4[2 * m + 1, i] = second

    def y_copy(d, source, device):
        return remote(s4.at[lax.rem(z + d, NZ)], gathered.at[view, source], y_s.at[d], y_r.at[d], device)

    @pl.loop(0, NZ - 1)
    def _(i):
        d = far_first(i)
        y_copy(d, z, at_z(lax.rem(z + d, NZ))).start()

    gathered[view, z] = s4[z]

    @pl.loop(0, NZ - 1)
    def _(i):
        d = far_first(i)
        y_copy(d, lax.rem(z + NZ - d, NZ), at_z(lax.rem(z + d, NZ))).wait_recv()

    def v_copy(m, source, device):
        return remote(gathered.at[source], gathered.at[source], v_s.at[m], v_r.at[m], device)

    for m in range(1, VIEWS):
        v_copy(m, view, at_view(lax.rem(view + m, VIEWS))).start()
    for m in range(1, VIEWS):
        v_copy(m, lax.rem(view + VIEWS - m, VIEWS), at_view(lax.rem(view + m, VIEWS))).wait_recv()

    @pl.loop(0, NZ)
    def _(zt):
        for h in range(2):
            for i in range(4):
                first, second = exchange_halves(gathered[2 * h, zt, i], gathered[2 * h + 1, zt, i])
                turned[64 * h + 16 * i : 64 * h + 16 * i + 8, :] = first
                turned[64 * h + 16 * i + 8 : 64 * h + 16 * i + 16, :] = second
        out[pl.ds(pl.multiple_of(BLOCK * zt, BLOCK), BLOCK), :] = turned[...].T

    for m in range(1, VIEWS):
        par_copy(m, view, at_view(lax.rem(view + m, VIEWS))).wait_send()
        v_copy(m, view, at_view(lax.rem(view + m, VIEWS))).wait_send()

    @pl.loop(1, NZ)
    def _(d):
        z_copy(d, z, at_z(lax.rem(z + d, NZ))).wait_send()
        y_copy(d, z, at_z(lax.rem(z + d, NZ))).wait_send()

    @pl.loop(1, 32)
    def _(n):
        to = lax.rem(place + n, 32)
        obs_copy(n, g_of(to), view, slab, at_place(to)).wait_send()

    @pl.loop(1, 8)
    def _(n):
        p_copy(n, lax.rem(kk + n, 8), kk).wait_send()
        q_copy(n, lax.rem(kk + n, 8), kk).wait_send()

    for it in range(ITERS):
        for copy in (*ext_columns(it), *ext_rows(it)):
            copy.wait_send()

        @pl.loop(0, VIEWS)
        def _(v):
            for copy in (*spread_columns(it, v), *tall_rows(it, v)):
                copy.wait_send()


def on_device(estimate, observed, long_taps, short_taps, brick_map, valid_rows):
    dma = pltpu.SemaphoreType.DMA
    vmem = pl.BlockSpec(memory_space=pltpu.VMEM)
    scratch = [
        ((VIEWS, 8, 128), F32),
        ((128, 128), F32),
        ((NZ, 4, 8, 128), F32),
        ((NZ, 4, 8, 128), F32),
        ((512, 128), F32),
        ((512, 128), F32),
        ((2048, 128), F32),
        ((VIEWS, 8, 64, 128), F32),
        ((ITERS, WIDE, TALL, 128), F32),
        ((WIDE, VIEWS * BLOCK, 128), F32),
        ((ITERS, VIEWS, WIDE, BLOCK, 128), F32),
        ((ITERS, VIEWS, OWN, TALL, 128), F32),
        ((VIEWS, OWN, BLOCK, 128), F32),
        ((512, 128), F32),
        ((8, 64, 128), F32),
        ((NZ, 4, 8, 128), F32),
        ((VIEWS, NZ, 4, 8, 128), F32),
        ((VIEWS * 8, 128), F32),
        *[((VIEWS, 128, 128), BF16)] * 4,
        *[((VIEWS * BLOCK, TALL), BF16)] * 4,
    ]
    semaphores = [
        (VIEWS,), (VIEWS,), (NZ,), (NZ,), (32,), (32,), (8,), (8,),
        (ITERS, 2), (ITERS, 2), (ITERS, 2), (ITERS, 2),
        (ITERS, VIEWS, 2), (ITERS, VIEWS, 2), (ITERS, VIEWS, 2), (ITERS, VIEWS, 2),
        (8,), (8,), (NZ,), (NZ,), (VIEWS,), (VIEWS,),
    ]
    refined = pl.pallas_call(
        kernel,
        out_shape=jax.ShapeDtypeStruct((ROWS, COLS), F32),
        in_specs=[vmem] * 6,
        out_specs=vmem,
        scratch_shapes=[pltpu.VMEM(s, t) for s, t in scratch] + [dma(s) for s in semaphores],
        compiler_params=pltpu.CompilerParams(
            collective_id=0, has_side_effects=True, vmem_limit_bytes=48 * 2**20
        ),
    )(
        estimate.reshape(ROWS, COLS),
        observed.reshape(BRICKS * 16, COLS),
        long_taps,
        short_taps.reshape(2, 7),
        brick_map,
        valid_rows,
    )
    return refined.reshape(1, ROWS, COLS)


def solution(mesh):
    fine = Mesh(mesh.devices.reshape(2, 2, NZ, NY, 2), AXES)
    view, bricks = ("xh", "core"), ("z", "y", "xl")
    placed = (
        P(bricks, None, None),
        P(view, None, bricks, None),
        P(view, None),
        P(view, None, None),
        P(view, None),
        P(view, None),
    )
    return jax.shard_map(
        on_device, mesh=fine, in_specs=placed, out_specs=P(bricks, None, None), check_vma=False
    )
```

```python
import jax
import jax.numpy as jnp
from jax import lax
from jax.experimental import pallas as pl
from jax.experimental.pallas import tpu as pltpu
from jax.sharding import Mesh
from jax.sharding import PartitionSpec as P

F32, BF16 = jnp.float32, jnp.bfloat16
ITERS = 2
VIEWS, BRICKS, ROWS, COLS = 4, 128, 2048, 128
NZ, NY = 16, 4
BLOCK = 128
OWN = 4
WIDE = OWN + 6
HALO = 16
TALL = BLOCK + 2 * HALO
AXES = ("xh", "core", "z", "y", "xl")
MESH = pl.DeviceIdType.MESH


def split(x):
    head = x.astype(BF16)
    return head, (x - head.astype(F32)).astype(BF16)


def dot3(ah, al, bh, bl):
    def dot(a, b):
        return jnp.dot(a, b, preferred_element_type=F32)

    return dot(ah, bh) + (dot(al, bh) + dot(ah, bl))


def exchange_halves(a, b):
    axis = a.ndim - 2
    top = lax.broadcasted_iota(jnp.int32, a.shape, axis) < 4
    first = jnp.where(top, a, pltpu.roll(b, 4, axis))
    second = jnp.where(top, pltpu.roll(a, 4, axis), b)
    return first, second


def loop(n, body):
    def step(i, carry):
        body(i)
        return carry

    lax.fori_loop(0, n, step, 0)


def kernel(
    est_ref, obs_ref, long_taps, short_taps, brick_map, valid_rows, out,
    est, obs, par, turned, s1, r1, s2, r2, obs_out, obs_in, ext, rows_done, spread, tall, corr,
    x2, r3, s4, gathered, tile_taps, bf_h, bf_l, bb_h, bb_l, tf_h, tf_l, tb_h, tb_l,
    par_s, par_r, z_s, z_r, obs_s, obs_r, p_s, p_r, e_s, e_r, uc_s, uc_r, ur_s, ur_r,
    q_s, q_r, y_s, y_r, core_s, core_r, mate_s, mate_r, next_s, next_r, in_s,
):
    xh, core, z, y, xl = (lax.axis_index(a) for a in AXES)
    x = 2 * xh + xl
    kk = 4 * xl + lax.rem(y + x, NY)
    k = 8 * xh + kk
    g = 2 * k + core
    view = 2 * xh + core
    slab = 2 * y + xl
    place = view * 8 + slab

    def at_kk(xh_, core_, kk_):
        xl_ = kk_ // 4
        return xh_, core_, z, lax.rem(lax.rem(kk_, 4) + 8 - 2 * xh_ - xl_, NY), xl_

    def slab_of(kk_):
        _, _, _, y_, xl_ = at_kk(xh, core, kk_)
        return 2 * y_ + xl_

    def at_g(g_, z_=None):
        k_ = g_ // 2
        xh_, core_, _, y_, xl_ = at_kk(k_ // 8, lax.rem(g_, 2), lax.rem(k_, 8))
        return xh_, core_, z if z_ is None else z_, y_, xl_

    def at_z(z_):
        return xh, core, z_, y, xl

    def at_place(place_):
        return place_ // 16, lax.rem(place_ // 8, 2), z, lax.rem(place_ // 2, 4), lax.rem(place_, 2)

    def at_view(view_):
        return view_ // 2, lax.rem(view_, 2), z, y, xl

    def g_of(place_):
        xh_, _, _, y_, xl_ = at_place(place_)
        x_ = 2 * xh_ + xl_
        return 2 * (4 * x_ + lax.rem(y_ + x_, NY)) + lax.rem(place_ // 8, 2)

    def remote(src, dst, send, recv, device):
        return pltpu.make_async_remote_copy(
            src_ref=src, dst_ref=dst, send_sem=send, recv_sem=recv, device_id=device, device_id_type=MESH
        )

    leaving = []

    def later(first, last, copy):
        def wait():
            @pl.loop(first, last)
            def _(i):
                copy(i).wait_send()

        leaving.append(wait)

    left, right = lax.rem(g + 31, 32), lax.rem(g + 1, 32)
    above, below = lax.rem(z + NZ - 1, NZ), lax.rem(z + 1, NZ)

    loads = [
        pltpu.make_async_copy(a, b, in_s.at[i]) for i, (a, b) in enumerate(((est_ref, est), (obs_ref, obs)))
    ]
    for load in loads:
        load.start()

    barrier = pltpu.get_barrier_semaphore()

    @pl.loop(1, NZ)
    def _(d):
        pl.semaphore_signal(barrier, inc=1, device_id=at_z(lax.rem(z + d, NZ)), device_id_type=MESH)

    @pl.loop(1, 32)
    def _(n):
        pl.semaphore_signal(barrier, inc=1, device_id=at_place(lax.rem(place + n, 32)), device_id_type=MESH)

    for g_ in (left, right):
        for z_ in (above, below):
            pl.semaphore_signal(barrier, inc=1, device_id=at_g(g_, z_), device_id_type=MESH)

    par[view] = jnp.zeros((8, 128), F32)
    par[view, 0:1, :] = brick_map[...].astype(F32)
    par[view, 1:2, :] = valid_rows[...].astype(F32)
    par[view, 2:3, 0:31] = long_taps[...]
    par[view, 3:5, 0:7] = short_taps[...]

    pl.semaphore_wait(barrier, NZ - 1 + 31 + 4)

    def par_copy(m, source, device):
        return remote(par.at[source], par.at[source], par_s.at[m], par_r.at[m], device)

    for m in range(1, VIEWS):
        par_copy(m, view, at_view(lax.rem(view + m, VIEWS))).start()
    later(1, VIEWS, lambda m: par_copy(m, view, at_view(lax.rem(view + m, VIEWS))))

    loads[0].wait()

    def piece_for(zt):
        block = est[pl.ds(pl.multiple_of(BLOCK * zt, BLOCK), BLOCK), :]
        turned[...] = block.T
        half = turned[pl.ds(pl.multiple_of(64 * xh, 64), 64), :].reshape(4, 2, 8, 128)
        first, second = exchange_halves(half[:, 0], half[:, 1])
        return jnp.where(core == 0, first, second)

    def z_copy(d, source, device):
        return remote(s1.at[d], r1.at[source], z_s.at[d], z_r.at[d], device)

    def far_first(i):
        return 8 + ((i + 1) // 2) * (1 - 2 * lax.rem(i, 2))

    @pl.loop(0, NZ - 1)
    def _(i):
        d = far_first(i)
        zt = lax.rem(z + d, NZ)
        s1[d] = piece_for(zt)
        z_copy(d, z, at_z(zt)).start()

    later(1, NZ, lambda d: z_copy(d, z, at_z(lax.rem(z + d, NZ))))
    r1[z] = piece_for(z)

    loads[1].wait()

    @pl.loop(0, 16)
    def _(r):
        obs_out[pl.ds(r, 128, stride=16), :] = obs[pl.ds(r, 128, stride=16), :].T

    def obs_copy(n, g_, view_, slab_, device):
        src = obs_out.at[pl.ds(pl.multiple_of(64 * g_, 64), 64)]
        return remote(src, obs_in.at[view_, slab_], obs_s.at[n], obs_r.at[n], device)

    @pl.loop(1, 32)
    def _(n):
        to = lax.rem(place + n, 32)
        obs_copy(n, g_of(to), view, slab, at_place(to)).start()

    def obs_sent(n):
        to = lax.rem(place + n, 32)
        return obs_copy(n, g_of(to), view, slab, at_place(to))

    later(1, 32, obs_sent)
    obs_in[view, slab] = obs_out[pl.ds(pl.multiple_of(64 * g, 64), 64), :]

    for m in range(1, VIEWS):
        par_copy(m, lax.rem(view + VIEWS - m, VIEWS), at_view(lax.rem(view + m, VIEWS))).wait_recv()
    lane = lax.broadcasted_iota(jnp.int32, (1, 128), 1)
    order = lax.broadcasted_iota(jnp.int32, (128, 128), 0)
    brick = (lax.rem(order, 16) * 8 + order // 16).astype(F32)
    tall_lane = lax.broadcasted_iota(jnp.int32, (BLOCK, TALL), 1)
    inside = jnp.logical_and(
        jnp.logical_or(tall_lane >= HALO, z > 0), jnp.logical_or(tall_lane < HALO + BLOCK, z < NZ - 1)
    )
    for v in range(VIEWS):
        bricks, long_row, plane, column = (par[v, i : i + 1, :] for i in (0, 2, 3, 4))
        long_row, plane, column = (t / jnp.sum(t, axis=1, keepdims=True) for t in (long_row, plane, column))
        matrix = jnp.zeros((128, 128), F32)
        for t in range(7):
            near = pltpu.roll(bricks, (3 - t) % 128, 1)
            near = jnp.where(jnp.logical_and(lane + (t - 3) >= 0, lane + (t - 3) < BRICKS), near, -1.0)
            matrix += jnp.where(brick == near, plane[:, t : t + 1], 0.0)
            tile_taps[8 * v + t : 8 * v + t + 1, :] = jnp.broadcast_to(column[:, t : t + 1], (1, 128))
        bf_h[v], bf_l[v] = split(matrix)
        bb_h[v], bb_l[v] = split(matrix.T)
        padded = jnp.concatenate([long_row, jnp.zeros((1, 128), F32)], axis=1)
        wide = jnp.broadcast_to(padded, (BLOCK, 256))
        toeplitz = pltpu.roll(wide, 1, 1, stride=1, stride_axis=0)[:, :TALL]
        tf_h[pl.ds(BLOCK * v, BLOCK), :], tf_l[pl.ds(BLOCK * v, BLOCK), :] = split(
            jnp.where(inside, toeplitz, 0.0)
        )
        high = jnp.broadcast_to(padded, (256, 256))
        flipped = pltpu.roll(high, 225, 1, stride=1, stride_axis=0)[:, :128].T[:, :TALL]
        tb_h[pl.ds(BLOCK * v, BLOCK), :], tb_l[pl.ds(BLOCK * v, BLOCK), :] = split(
            jnp.where(inside, flipped, 0.0)
        )

    @pl.loop(0, NZ - 1)
    def _(i):
        d = far_first(i)
        z_copy(d, lax.rem(z + NZ - d, NZ), at_z(lax.rem(z + d, NZ))).wait_recv()

    @pl.loop(0, 8)
    def _(m):
        first, second = exchange_halves(r1[2 * m], r1[2 * m + 1])
        for i in range(4):
            s2[pl.ds(pl.multiple_of(64 * (2 * i) + 8 * m, 8), 8), :] = first[i]
            s2[pl.ds(pl.multiple_of(64 * (2 * i + 1) + 8 * m, 8), 8), :] = second[i]

    def p_copy(n, kt, source):
        src = s2.at[pl.ds(pl.multiple_of(64 * kt, 64), 64)]
        dst = r2.at[pl.ds(pl.multiple_of(64 * slab_of(source), 64), 64)]
        return remote(src, dst, p_s.at[n], p_r.at[n], at_kk(xh, core, kt))

    @pl.loop(1, 8)
    def _(n):
        p_copy(n, lax.rem(kk + n, 8), kk).start()

    later(1, 8, lambda n: p_copy(n, lax.rem(kk + n, 8), kk))
    mine = pl.ds(pl.multiple_of(64 * slab, 64), 64)
    r2[mine, :] = s2[pl.ds(pl.multiple_of(64 * kk, 64), 64), :]

    @pl.loop(1, 8)
    def _(n):
        p_copy(n, lax.rem(kk + n, 8), lax.rem(kk + 8 - n, 8)).wait_recv()

    for c in range(OWN):
        ext[0, 3 + c, HALO : HALO + BLOCK, :] = r2[pl.ds(c, 128, stride=4), :].T

    def observed_arrives():
        @pl.loop(1, 32)
        def _(n):
            source = lax.rem(place + 32 - n, 32)
            to = lax.rem(place + n, 32)
            obs_copy(n, g_of(to), source // 8, lax.rem(source, 8), at_place(to)).wait_recv()

    middle = pl.ds(HALO, BLOCK)

    first, last = pl.ds(HALO, HALO), pl.ds(BLOCK, HALO)
    before, after = pl.ds(0, HALO), pl.ds(HALO + BLOCK, HALO)

    def ext_copy(it, i, columns, rows, to_columns, to_rows, device):
        return remote(
            ext.at[it, columns, rows], ext.at[it, to_columns, to_rows], e_s.at[it, i], e_r.at[it, i], device
        )

    def ext_sides(it):
        return (
            ext_copy(it, 0, pl.ds(3, 3), middle, pl.ds(7, 3), middle, at_g(left)),
            ext_copy(it, 1, pl.ds(4, 3), middle, pl.ds(0, 3), middle, at_g(right)),
            ext_copy(it, 2, pl.ds(3, 3), first, pl.ds(7, 3), after, at_g(left, above)),
            ext_copy(it, 3, pl.ds(3, 3), last, pl.ds(7, 3), before, at_g(left, below)),
            ext_copy(it, 4, pl.ds(4, 3), first, pl.ds(0, 3), after, at_g(right, above)),
            ext_copy(it, 5, pl.ds(4, 3), last, pl.ds(0, 3), before, at_g(right, below)),
        )

    def ext_rows(it):
        own = pl.ds(3, OWN)
        return (
            ext_copy(it, 6, own, first, own, after, at_z(above)),
            ext_copy(it, 7, own, last, own, before, at_z(below)),
        )

    def spread_columns(it, v):
        return (
            remote(spread.at[it, v, 3:6], spread.at[it, v, 7:10], uc_s.at[it, v, 0], uc_r.at[it, v, 0], at_g(left)),
            remote(spread.at[it, v, 4:7], spread.at[it, v, 0:3], uc_s.at[it, v, 1], uc_r.at[it, v, 1], at_g(right)),
        )

    def tall_rows(it, v):
        return (
            remote(tall.at[it, v, :, first], tall.at[it, v, :, after], ur_s.at[it, v, 0], ur_r.at[it, v, 0], at_z(above)),
            remote(tall.at[it, v, :, last], tall.at[it, v, :, before], ur_s.at[it, v, 1], ur_r.at[it, v, 1], at_z(below)),
        )

    def column_inside(i):
        at = OWN * g + i - 3
        return jnp.logical_and(at >= 0, at < COLS)

    row_ids = (BLOCK * z + lax.broadcasted_iota(jnp.int32, (BLOCK, 128), 0)).astype(F32)

    def send(copies):
        for copy in copies:
            copy.start()

    def arrive(copies):
        for copy in copies:
            copy.wait_recv()

    def blur_rows(it, i):
        head, tail = split(jnp.where(column_inside(i), ext[it, i], 0.0))
        rows_done[i] = dot3(tf_h[...], tf_l[...], head, tail)

    def back_projected(v, c):
        part = pl.ds(pl.multiple_of(BLOCK * v, BLOCK), BLOCK)
        blurred = jnp.zeros((BLOCK, 128), F32)
        for t in range(7):
            blurred += tile_taps[pl.ds(8 * v + t, 1), :] * rows_done[c + t, part, :]
        blurred = dot3(*split(blurred), bf_h[v], bf_l[v])
        seen = obs_in[v, :, pl.ds(pl.multiple_of(16 * c, 16), 16), :].reshape(BLOCK, 128)
        ratio = jnp.where(row_ids < par[v, 1:2, :], seen / blurred, 1.0)
        return dot3(*split(ratio), bb_h[v], bb_l[v])

    def columns_back(it, v, c):
        total = jnp.zeros((BLOCK, 128), F32)
        for t in range(7):
            tap = jnp.where(column_inside(c + t), tile_taps[pl.ds(8 * v + 6 - t, 1), :], 0.0)
            total += tap * spread[it, v, c + t]
        return total

    def rows_back(it, v, c):
        part = pl.ds(pl.multiple_of(BLOCK * v, BLOCK), BLOCK)
        return dot3(tb_h[part, :], tb_l[part, :], *split(tall[it, v, c]))

    for it in range(ITERS):
        send(ext_sides(it))
        send(ext_rows(it))
        leaving.extend(copy.wait_send for copy in (*ext_sides(it), *ext_rows(it)))
        arrive(ext_rows(it))

        @pl.loop(3, 3 + OWN)
        def _(i):
            blur_rows(it, i)

        arrive(ext_sides(it))

        @pl.loop(0, 6)
        def _(i):
            blur_rows(it, i + OWN * (i // 3))

        if it == 0:
            observed_arrives()

        @pl.loop(0, 2)
        def _(v):
            @pl.loop(0, OWN)
            def _(c):
                spread[it, v, 3 + c] = back_projected(v, c)

            send(spread_columns(it, v))

        @pl.loop(2, VIEWS)
        def _(v):
            @pl.loop(0, OWN)
            def _(c):
                tall[it, v, c, HALO : HALO + BLOCK, :] = back_projected(v, c)

            send(tall_rows(it, v))

        @pl.loop(2, VIEWS)
        def _(v):
            arrive(tall_rows(it, v))

            @pl.loop(0, OWN)
            def _(c):
                spread[it, v, 3 + c] = rows_back(it, v, c)

            send(spread_columns(it, v))

        @pl.loop(0, 2)
        def _(v):
            arrive(spread_columns(it, v))

            @pl.loop(0, OWN)
            def _(c):
                tall[it, v, c, HALO : HALO + BLOCK, :] = columns_back(it, v, c)

            send(tall_rows(it, v))

        @pl.loop(0, 2)
        def _(v):
            arrive(tall_rows(it, v))

            @pl.loop(0, OWN)
            def _(c):
                corr[v, c] = rows_back(it, v, c)

        @pl.loop(2, VIEWS)
        def _(v):
            arrive(spread_columns(it, v))

            @pl.loop(0, OWN)
            def _(c):
                corr[v, c] = columns_back(it, v, c)

        for i in range(2):
            later(0, VIEWS, lambda v, i=i, it=it: spread_columns(it, v)[i])
            later(0, VIEWS, lambda v, i=i, it=it: tall_rows(it, v)[i])

        for c in range(OWN):
            log_total = jnp.log(corr[0, c] * corr[1, c]) + jnp.log(corr[2, c] * corr[3, c])
            current = ext[it, 3 + c, HALO : HALO + BLOCK, :] * jnp.exp(log_total)
            if it < ITERS - 1:
                ext[it + 1, 3 + c, HALO : HALO + BLOCK, :] = current
            else:
                x2[pl.ds(c, 128, stride=4), :] = current.T

    def q_copy(n, kt, source):
        src = x2.at[pl.ds(pl.multiple_of(64 * slab_of(kt), 64), 64)]
        return remote(src, r3.at[source], q_s.at[n], q_r.at[n], at_kk(xh, core, kt))

    @pl.loop(1, 8)
    def _(n):
        q_copy(n, lax.rem(kk + n, 8), kk).start()

    later(1, 8, lambda n: q_copy(n, lax.rem(kk + n, 8), kk))
    r3[kk] = x2[mine, :]

    @pl.loop(1, 8)
    def _(n):
        q_copy(n, lax.rem(kk + n, 8), lax.rem(kk + 8 - n, 8)).wait_recv()

    @pl.loop(0, 8)
    def _(m):
        part = pl.ds(pl.multiple_of(8 * m, 8), 8)
        for i in range(4):
            first, second = exchange_halves(r3[2 * i, part, :], r3[2 * i + 1, part, :])
            s4[2 * m, i] = first
            s4[2 * m + 1, i] = second

    def y_copy(i, device):
        d = far_first(i - 1)
        return remote(s4.at[lax.rem(z + d, NZ)], gathered.at[view, i], y_s.at[i], y_r.at[i], device)

    def y_sent(i):
        return y_copy(i, at_z(lax.rem(z + far_first(i - 1), NZ)))

    @pl.loop(1, NZ)
    def _(i):
        y_sent(i).start()

    later(1, NZ, y_sent)
    gathered[view, 0] = s4[z]

    other_core, other_chip = (xh, 1 - core, z, y, xl), (1 - xh, core, z, y, xl)
    over = 2 * (1 - xh) + core

    def pass_on(j, owner, send_sem, recv_sem, device):
        blocks = gathered.at[owner, pl.ds(pl.multiple_of(4 * j, 4), 4)]
        return remote(blocks, blocks, send_sem.at[j], recv_sem.at[j], device)

    def to_core(j):
        return pass_on(j, view, core_s, core_r, other_core)

    def to_chip(j):
        return pass_on(j, view, mate_s, mate_r, other_chip)

    def onward(j):
        return pass_on(j, over, next_s, next_r, other_core)

    for copy in (to_core, to_chip, onward):
        later(0, NZ // 4, copy)

    def finish(j):
        pass_on(j, 2 * xh + 1 - core, core_s, core_r, other_core).wait_recv()
        pass_on(j, 2 * (1 - xh) + 1 - core, next_s, next_r, other_core).wait_recv()

        @pl.loop(0, 4)
        def _(n):
            i = 4 * j + n
            zt = lax.rem(z + NZ - jnp.where(i == 0, 0, far_first(i - 1)), NZ)
            for h in range(2):
                for t in range(4):
                    a, b = exchange_halves(gathered[2 * h, i, t], gathered[2 * h + 1, i, t])
                    turned[64 * h + 16 * t : 64 * h + 16 * t + 8, :] = a
                    turned[64 * h + 16 * t + 8 : 64 * h + 16 * t + 16, :] = b
            out[pl.ds(pl.multiple_of(BLOCK * zt, BLOCK), BLOCK), :] = turned[...].T

    @pl.loop(0, NZ // 4)
    def _(j):
        @pl.loop(jnp.where(j == 0, 1, 4 * j), 4 * j + 4)
        def _(i):
            y_sent(i).wait_recv()

        to_chip(j).start()
        to_core(j).start()

        @pl.when(j > 0)
        def _():
            pass_on(j - 1, over, mate_s, mate_r, other_chip).wait_recv()
            onward(j - 1).start()

    end = NZ // 4 - 1
    pass_on(end, over, mate_s, mate_r, other_chip).wait_recv()
    onward(end).start()

    @pl.loop(0, NZ // 4)
    def _(j):
        finish(j)

    for wait in leaving:
        wait()


def on_device(estimate, observed, long_taps, short_taps, brick_map, valid_rows):
    dma = pltpu.SemaphoreType.DMA
    vmem = pl.BlockSpec(memory_space=pltpu.VMEM)
    scratch = [
        ((ROWS, COLS), F32),
        ((ROWS, COLS), F32),
        ((VIEWS, 8, 128), F32),
        ((128, 128), F32),
        ((NZ, 4, 8, 128), F32),
        ((NZ, 4, 8, 128), F32),
        ((512, 128), F32),
        ((512, 128), F32),
        ((2048, 128), F32),
        ((VIEWS, 8, 64, 128), F32),
        ((ITERS, WIDE, TALL, 128), F32),
        ((WIDE, VIEWS * BLOCK, 128), F32),
        ((ITERS, VIEWS, WIDE, BLOCK, 128), F32),
        ((ITERS, VIEWS, OWN, TALL, 128), F32),
        ((VIEWS, OWN, BLOCK, 128), F32),
        ((512, 128), F32),
        ((8, 64, 128), F32),
        ((NZ, 4, 8, 128), F32),
        ((VIEWS, NZ, 4, 8, 128), F32),
        ((VIEWS * 8, 128), F32),
        *[((VIEWS, 128, 128), BF16)] * 4,
        *[((VIEWS * BLOCK, TALL), BF16)] * 4,
    ]
    semaphores = [
        (VIEWS,), (VIEWS,), (NZ,), (NZ,), (32,), (32,), (8,), (8,),
        (ITERS, 8), (ITERS, 8),
        (ITERS, VIEWS, 2), (ITERS, VIEWS, 2), (ITERS, VIEWS, 2), (ITERS, VIEWS, 2),
        (8,), (8,), (NZ,), (NZ,), (4,), (4,), (4,), (4,), (4,), (4,), (2,),
    ]
    refined = pl.pallas_call(
        kernel,
        out_shape=jax.ShapeDtypeStruct((ROWS, COLS), F32),
        in_specs=[pl.BlockSpec(memory_space=pl.ANY)] * 2 + [vmem] * 4,
        out_specs=vmem,
        scratch_shapes=[pltpu.VMEM(s, t) for s, t in scratch] + [dma(s) for s in semaphores],
        compiler_params=pltpu.CompilerParams(
            collective_id=0, has_side_effects=True, vmem_limit_bytes=56 * 2**20
        ),
    )(
        estimate.reshape(ROWS, COLS),
        observed.reshape(BRICKS * 16, COLS),
        long_taps,
        short_taps.reshape(2, 7),
        brick_map,
        valid_rows,
    )
    return refined.reshape(1, ROWS, COLS)


def solution(mesh):
    fine = Mesh(mesh.devices.reshape(2, 2, NZ, NY, 2), AXES)
    view, bricks = ("xh", "core"), ("z", "y", "xl")
    placed = (
        P(bricks, None, None),
        P(view, None, bricks, None),
        P(view, None),
        P(view, None, None),
        P(view, None),
        P(view, None),
    )
    return jax.shard_map(
        on_device, mesh=fine, in_specs=placed, out_specs=P(bricks, None, None), check_vma=False
    )
```

```python
import jax
import jax.numpy as jnp
from jax import lax
from jax.experimental import pallas as pl
from jax.experimental.pallas import tpu as pltpu
from jax.sharding import Mesh
from jax.sharding import PartitionSpec as P

F32, BF16 = jnp.float32, jnp.bfloat16
ITERS = 2
VIEWS, BRICKS, ROWS, COLS = 4, 128, 2048, 128
NZ, NY = 16, 4
BLOCK = 128
OWN = 4
WIDE = OWN + 6
HALO = 16
TALL = BLOCK + 2 * HALO
AXES = ("xh", "core", "z", "y", "xl")
MESH = pl.DeviceIdType.MESH


def split(x):
    head = x.astype(BF16)
    return head, (x - head.astype(F32)).astype(BF16)


def dot3(ah, al, bh, bl):
    def dot(a, b):
        return jnp.dot(a, b, preferred_element_type=F32)

    return dot(ah, bh) + (dot(al, bh) + dot(ah, bl))


def doubled(matrix):
    head, tail = split(matrix)
    return jnp.concatenate(
        [jnp.concatenate([head, tail], axis=1), jnp.concatenate([head, jnp.zeros_like(tail)], axis=1)], axis=0
    )


def product(x, twice):
    both = jnp.dot(jnp.concatenate(split(x), axis=1), twice, preferred_element_type=F32)
    return both[:, :128] + both[:, 128:]


def exchange_halves(a, b):
    axis = a.ndim - 2
    top = lax.broadcasted_iota(jnp.int32, a.shape, axis) < 4
    first = jnp.where(top, a, pltpu.roll(b, 4, axis))
    second = jnp.where(top, pltpu.roll(a, 4, axis), b)
    return first, second


def loop(n, body):
    def step(i, carry):
        body(i)
        return carry

    lax.fori_loop(0, n, step, 0)


def kernel(
    est_ref, obs_ref, long_taps, short_taps, brick_map, valid_rows, out,
    est, obs, par, turned, s1, r1, s2, r2, obs_out, obs_in, ext, rows_done, spread, tall, corr,
    x2, r3, s4, gathered, tile_taps, ahead, back, tf_h, tf_l, tb_h, tb_l,
    par_s, par_r, z_s, z_r, obs_s, obs_r, p_s, p_r, e_s, e_r, uc_s, uc_r, ur_s, ur_r,
    q_s, q_r, y_s, y_r, core_s, core_r, mate_s, mate_r, next_s, next_r, in_s,
):
    xh, core, z, y, xl = (lax.axis_index(a) for a in AXES)
    x = 2 * xh + xl
    kk = 4 * xl + lax.rem(y + x, NY)
    k = 8 * xh + kk
    g = 2 * k + core
    view = 2 * xh + core
    slab = 2 * y + xl
    place = view * 8 + slab

    def at_kk(xh_, core_, kk_):
        xl_ = kk_ // 4
        return xh_, core_, z, lax.rem(lax.rem(kk_, 4) + 8 - 2 * xh_ - xl_, NY), xl_

    def slab_of(kk_):
        _, _, _, y_, xl_ = at_kk(xh, core, kk_)
        return 2 * y_ + xl_

    def at_g(g_, z_=None):
        k_ = g_ // 2
        xh_, core_, _, y_, xl_ = at_kk(k_ // 8, lax.rem(g_, 2), lax.rem(k_, 8))
        return xh_, core_, z if z_ is None else z_, y_, xl_

    def at_z(z_):
        return xh, core, z_, y, xl

    def at_place(place_):
        return place_ // 16, lax.rem(place_ // 8, 2), z, lax.rem(place_ // 2, 4), lax.rem(place_, 2)

    def at_view(view_):
        return view_ // 2, lax.rem(view_, 2), z, y, xl

    def g_of(place_):
        xh_, _, _, y_, xl_ = at_place(place_)
        x_ = 2 * xh_ + xl_
        return 2 * (4 * x_ + lax.rem(y_ + x_, NY)) + lax.rem(place_ // 8, 2)

    def remote(src, dst, send, recv, device):
        return pltpu.make_async_remote_copy(
            src_ref=src, dst_ref=dst, send_sem=send, recv_sem=recv, device_id=device, device_id_type=MESH
        )

    leaving = []

    def later(first, last, copy):
        def wait():
            @pl.loop(first, last)
            def _(i):
                copy(i).wait_send()

        leaving.append(wait)

    left, right = lax.rem(g + 31, 32), lax.rem(g + 1, 32)
    above, below = lax.rem(z + NZ - 1, NZ), lax.rem(z + 1, NZ)

    loads = [
        pltpu.make_async_copy(a, b, in_s.at[i]) for i, (a, b) in enumerate(((est_ref, est), (obs_ref, obs)))
    ]
    for load in loads:
        load.start()

    barrier = pltpu.get_barrier_semaphore()

    @pl.loop(1, NZ)
    def _(d):
        pl.semaphore_signal(barrier, inc=1, device_id=at_z(lax.rem(z + d, NZ)), device_id_type=MESH)

    @pl.loop(1, 32)
    def _(n):
        pl.semaphore_signal(barrier, inc=1, device_id=at_place(lax.rem(place + n, 32)), device_id_type=MESH)

    for g_ in (left, right):
        for z_ in (above, below):
            pl.semaphore_signal(barrier, inc=1, device_id=at_g(g_, z_), device_id_type=MESH)

    par[view] = jnp.zeros((8, 128), F32)
    par[view, 0:1, :] = brick_map[...].astype(F32)
    par[view, 1:2, :] = valid_rows[...].astype(F32)
    par[view, 2:3, 0:31] = long_taps[...]
    par[view, 3:5, 0:7] = short_taps[...]

    pl.semaphore_wait(barrier, NZ - 1 + 31 + 4)

    def par_copy(m, source, device):
        return remote(par.at[source], par.at[source], par_s.at[m], par_r.at[m], device)

    for m in range(1, VIEWS):
        par_copy(m, view, at_view(lax.rem(view + m, VIEWS))).start()
    later(1, VIEWS, lambda m: par_copy(m, view, at_view(lax.rem(view + m, VIEWS))))

    loads[0].wait()

    def piece_for(zt):
        block = est[pl.ds(pl.multiple_of(BLOCK * zt, BLOCK), BLOCK), :]
        turned[...] = block.T
        half = turned[pl.ds(pl.multiple_of(64 * xh, 64), 64), :].reshape(4, 2, 8, 128)
        first, second = exchange_halves(half[:, 0], half[:, 1])
        return jnp.where(core == 0, first, second)

    def z_copy(d, source, device):
        return remote(s1.at[d], r1.at[source], z_s.at[d], z_r.at[d], device)

    def far_first(i):
        return 8 + ((i + 1) // 2) * (1 - 2 * lax.rem(i, 2))

    @pl.loop(0, NZ - 1)
    def _(i):
        d = far_first(i)
        zt = lax.rem(z + d, NZ)
        s1[d] = piece_for(zt)
        z_copy(d, z, at_z(zt)).start()

    later(1, NZ, lambda d: z_copy(d, z, at_z(lax.rem(z + d, NZ))))
    r1[z] = piece_for(z)

    loads[1].wait()

    @pl.loop(0, 16)
    def _(r):
        obs_out[pl.ds(r, 128, stride=16), :] = obs[pl.ds(r, 128, stride=16), :].T

    def obs_copy(n, g_, view_, slab_, device):
        src = obs_out.at[pl.ds(pl.multiple_of(64 * g_, 64), 64)]
        return remote(src, obs_in.at[view_, slab_], obs_s.at[n], obs_r.at[n], device)

    @pl.loop(1, 32)
    def _(n):
        to = lax.rem(place + n, 32)
        obs_copy(n, g_of(to), view, slab, at_place(to)).start()

    def obs_sent(n):
        to = lax.rem(place + n, 32)
        return obs_copy(n, g_of(to), view, slab, at_place(to))

    later(1, 32, obs_sent)
    obs_in[view, slab] = obs_out[pl.ds(pl.multiple_of(64 * g, 64), 64), :]

    for m in range(1, VIEWS):
        par_copy(m, lax.rem(view + VIEWS - m, VIEWS), at_view(lax.rem(view + m, VIEWS))).wait_recv()
    lane = lax.broadcasted_iota(jnp.int32, (1, 128), 1)
    order = lax.broadcasted_iota(jnp.int32, (128, 128), 0)
    brick = (lax.rem(order, 16) * 8 + order // 16).astype(F32)
    tall_lane = lax.broadcasted_iota(jnp.int32, (BLOCK, TALL), 1)
    inside = jnp.logical_and(
        jnp.logical_or(tall_lane >= HALO, z > 0), jnp.logical_or(tall_lane < HALO + BLOCK, z < NZ - 1)
    )
    for v in range(VIEWS):
        bricks, long_row, plane, column = (par[v, i : i + 1, :] for i in (0, 2, 3, 4))
        long_row, plane, column = (t / jnp.sum(t, axis=1, keepdims=True) for t in (long_row, plane, column))
        matrix = jnp.zeros((128, 128), F32)
        for t in range(7):
            near = pltpu.roll(bricks, (3 - t) % 128, 1)
            near = jnp.where(jnp.logical_and(lane + (t - 3) >= 0, lane + (t - 3) < BRICKS), near, -1.0)
            matrix += jnp.where(brick == near, plane[:, t : t + 1], 0.0)
            tile_taps[8 * v + t : 8 * v + t + 1, :] = jnp.broadcast_to(column[:, t : t + 1], (1, 128))
        ahead[v], back[v] = doubled(matrix), doubled(matrix.T)
        padded = jnp.concatenate([long_row, jnp.zeros((1, 128), F32)], axis=1)
        wide = jnp.broadcast_to(padded, (BLOCK, 256))
        toeplitz = pltpu.roll(wide, 1, 1, stride=1, stride_axis=0)[:, :TALL]
        tf_h[pl.ds(BLOCK * v, BLOCK), :], tf_l[pl.ds(BLOCK * v, BLOCK), :] = split(
            jnp.where(inside, toeplitz, 0.0)
        )
        high = jnp.broadcast_to(padded, (256, 256))
        flipped = pltpu.roll(high, 225, 1, stride=1, stride_axis=0)[:, :128].T[:, :TALL]
        tb_h[pl.ds(BLOCK * v, BLOCK), :], tb_l[pl.ds(BLOCK * v, BLOCK), :] = split(
            jnp.where(inside, flipped, 0.0)
        )

    @pl.loop(0, NZ - 1)
    def _(i):
        d = far_first(i)
        z_copy(d, lax.rem(z + NZ - d, NZ), at_z(lax.rem(z + d, NZ))).wait_recv()

    @pl.loop(0, 8)
    def _(m):
        first, second = exchange_halves(r1[2 * m], r1[2 * m + 1])
        for i in range(4):
            s2[pl.ds(pl.multiple_of(64 * (2 * i) + 8 * m, 8), 8), :] = first[i]
            s2[pl.ds(pl.multiple_of(64 * (2 * i + 1) + 8 * m, 8), 8), :] = second[i]

    def p_copy(n, kt, source):
        src = s2.at[pl.ds(pl.multiple_of(64 * kt, 64), 64)]
        dst = r2.at[pl.ds(pl.multiple_of(64 * slab_of(source), 64), 64)]
        return remote(src, dst, p_s.at[n], p_r.at[n], at_kk(xh, core, kt))

    @pl.loop(1, 8)
    def _(n):
        p_copy(n, lax.rem(kk + n, 8), kk).start()

    later(1, 8, lambda n: p_copy(n, lax.rem(kk + n, 8), kk))
    mine = pl.ds(pl.multiple_of(64 * slab, 64), 64)
    r2[mine, :] = s2[pl.ds(pl.multiple_of(64 * kk, 64), 64), :]

    @pl.loop(1, 8)
    def _(n):
        p_copy(n, lax.rem(kk + n, 8), lax.rem(kk + 8 - n, 8)).wait_recv()

    for c in range(OWN):
        ext[0, 3 + c, HALO : HALO + BLOCK, :] = r2[pl.ds(c, 128, stride=4), :].T

    def observed_arrives():
        @pl.loop(1, 32)
        def _(n):
            source = lax.rem(place + 32 - n, 32)
            to = lax.rem(place + n, 32)
            obs_copy(n, g_of(to), source // 8, lax.rem(source, 8), at_place(to)).wait_recv()

    middle = pl.ds(HALO, BLOCK)

    first, last = pl.ds(HALO, HALO), pl.ds(BLOCK, HALO)
    before, after = pl.ds(0, HALO), pl.ds(HALO + BLOCK, HALO)

    def ext_copy(it, i, columns, rows, to_columns, to_rows, device):
        return remote(
            ext.at[it, columns, rows], ext.at[it, to_columns, to_rows], e_s.at[it, i], e_r.at[it, i], device
        )

    def ext_sides(it):
        return (
            ext_copy(it, 0, pl.ds(3, 3), middle, pl.ds(7, 3), middle, at_g(left)),
            ext_copy(it, 1, pl.ds(4, 3), middle, pl.ds(0, 3), middle, at_g(right)),
            ext_copy(it, 2, pl.ds(3, 3), first, pl.ds(7, 3), after, at_g(left, above)),
            ext_copy(it, 3, pl.ds(3, 3), last, pl.ds(7, 3), before, at_g(left, below)),
            ext_copy(it, 4, pl.ds(4, 3), first, pl.ds(0, 3), after, at_g(right, above)),
            ext_copy(it, 5, pl.ds(4, 3), last, pl.ds(0, 3), before, at_g(right, below)),
        )

    def ext_rows(it):
        own = pl.ds(3, OWN)
        return (
            ext_copy(it, 6, own, first, own, after, at_z(above)),
            ext_copy(it, 7, own, last, own, before, at_z(below)),
        )

    def spread_columns(it, v):
        return (
            remote(spread.at[it, v, 3:6], spread.at[it, v, 7:10], uc_s.at[it, v, 0], uc_r.at[it, v, 0], at_g(left)),
            remote(spread.at[it, v, 4:7], spread.at[it, v, 0:3], uc_s.at[it, v, 1], uc_r.at[it, v, 1], at_g(right)),
        )

    def tall_rows(it, v):
        return (
            remote(tall.at[it, v, :, first], tall.at[it, v, :, after], ur_s.at[it, v, 0], ur_r.at[it, v, 0], at_z(above)),
            remote(tall.at[it, v, :, last], tall.at[it, v, :, before], ur_s.at[it, v, 1], ur_r.at[it, v, 1], at_z(below)),
        )

    def column_inside(i):
        at = OWN * g + i - 3
        return jnp.logical_and(at >= 0, at < COLS)

    row_ids = (BLOCK * z + lax.broadcasted_iota(jnp.int32, (BLOCK, 128), 0)).astype(F32)

    def send(copies):
        for copy in copies:
            copy.start()

    def arrive(copies):
        for copy in copies:
            copy.wait_recv()

    def blur_rows(it, i, j):
        pair = jnp.concatenate([jnp.where(column_inside(n), ext[it, n], 0.0) for n in (i, j)], axis=1)
        done = dot3(tf_h[...], tf_l[...], *split(pair))
        rows_done[i], rows_done[j] = done[:, :128], done[:, 128:]

    def back_projected(v):
        part = pl.ds(pl.multiple_of(BLOCK * v, BLOCK), BLOCK)
        taps = [tile_taps[pl.ds(8 * v + t, 1), :] for t in range(7)]
        blurred = jnp.concatenate(
            [sum(taps[t] * rows_done[c + t, part, :] for t in range(7)) for c in range(OWN)], axis=0
        )
        blurred = product(blurred, ahead[v])
        ratios = []
        for c in range(OWN):
            seen = obs_in[v, :, 16 * c : 16 * c + 16, :].reshape(BLOCK, 128)
            ratio = seen / blurred[BLOCK * c : BLOCK * c + BLOCK]
            ratios.append(jnp.where(row_ids < par[v, 1:2, :], ratio, 1.0))
        return product(jnp.concatenate(ratios, axis=0), back[v]).reshape(OWN, BLOCK, 128)

    def columns_back(it, v, c):
        total = jnp.zeros((BLOCK, 128), F32)
        for t in range(7):
            tap = jnp.where(column_inside(c + t), tile_taps[pl.ds(8 * v + 6 - t, 1), :], 0.0)
            total += tap * spread[it, v, c + t]
        return total

    def rows_back(it, v):
        part = pl.ds(pl.multiple_of(BLOCK * v, BLOCK), BLOCK)
        beside = jnp.concatenate([tall[it, v, c] for c in range(OWN)], axis=1)
        done = dot3(tb_h[part, :], tb_l[part, :], *split(beside))
        return [done[:, 128 * c : 128 * c + 128] for c in range(OWN)]

    for it in range(ITERS):
        send(ext_sides(it))
        send(ext_rows(it))
        leaving.extend(copy.wait_send for copy in (*ext_sides(it), *ext_rows(it)))
        arrive(ext_rows(it))

        @pl.loop(0, 2)
        def _(i):
            blur_rows(it, 3 + 2 * i, 4 + 2 * i)

        arrive(ext_sides(it))

        @pl.loop(0, 3)
        def _(i):
            blur_rows(it, 2 * i + 4 * (i // 2), 1 + 6 * ((i + 1) // 2) + 2 * (i // 2))

        if it == 0:
            observed_arrives()

        @pl.loop(0, 2)
        def _(v):
            spread[it, v, 3 : 3 + OWN] = back_projected(v)
            send(spread_columns(it, v))

        @pl.loop(2, VIEWS)
        def _(v):
            tall[it, v, :, HALO : HALO + BLOCK, :] = back_projected(v)
            send(tall_rows(it, v))

        @pl.loop(2, VIEWS)
        def _(v):
            arrive(tall_rows(it, v))

            for c, done in enumerate(rows_back(it, v)):
                spread[it, v, 3 + c] = done
            send(spread_columns(it, v))

        @pl.loop(0, 2)
        def _(v):
            arrive(spread_columns(it, v))

            @pl.loop(0, OWN)
            def _(c):
                tall[it, v, c, HALO : HALO + BLOCK, :] = columns_back(it, v, c)

            send(tall_rows(it, v))

        @pl.loop(0, 2)
        def _(v):
            arrive(tall_rows(it, v))

            for c, done in enumerate(rows_back(it, v)):
                corr[v, c] = done

        @pl.loop(2, VIEWS)
        def _(v):
            arrive(spread_columns(it, v))

            @pl.loop(0, OWN)
            def _(c):
                corr[v, c] = columns_back(it, v, c)

        for i in range(2):
            later(0, VIEWS, lambda v, i=i, it=it: spread_columns(it, v)[i])
            later(0, VIEWS, lambda v, i=i, it=it: tall_rows(it, v)[i])

        for c in range(OWN):
            log_total = jnp.log(corr[0, c] * corr[1, c]) + jnp.log(corr[2, c] * corr[3, c])
            current = ext[it, 3 + c, HALO : HALO + BLOCK, :] * jnp.exp(log_total)
            if it < ITERS - 1:
                ext[it + 1, 3 + c, HALO : HALO + BLOCK, :] = current
            else:
                x2[pl.ds(c, 128, stride=4), :] = current.T

    def q_copy(n, kt, source):
        src = x2.at[pl.ds(pl.multiple_of(64 * slab_of(kt), 64), 64)]
        return remote(src, r3.at[source], q_s.at[n], q_r.at[n], at_kk(xh, core, kt))

    @pl.loop(1, 8)
    def _(n):
        q_copy(n, lax.rem(kk + n, 8), kk).start()

    later(1, 8, lambda n: q_copy(n, lax.rem(kk + n, 8), kk))
    r3[kk] = x2[mine, :]

    @pl.loop(1, 8)
    def _(n):
        q_copy(n, lax.rem(kk + n, 8), lax.rem(kk + 8 - n, 8)).wait_recv()

    @pl.loop(0, 8)
    def _(m):
        part = pl.ds(pl.multiple_of(8 * m, 8), 8)
        for i in range(4):
            first, second = exchange_halves(r3[2 * i, part, :], r3[2 * i + 1, part, :])
            s4[2 * m, i] = first
            s4[2 * m + 1, i] = second

    def y_copy(i, device):
        d = far_first(i - 1)
        return remote(s4.at[lax.rem(z + d, NZ)], gathered.at[view, i], y_s.at[i], y_r.at[i], device)

    def y_sent(i):
        return y_copy(i, at_z(lax.rem(z + far_first(i - 1), NZ)))

    @pl.loop(1, NZ)
    def _(i):
        y_sent(i).start()

    later(1, NZ, y_sent)
    gathered[view, 0] = s4[z]

    other_core, other_chip = (xh, 1 - core, z, y, xl), (1 - xh, core, z, y, xl)
    over = 2 * (1 - xh) + core

    def pass_on(j, owner, send_sem, recv_sem, device):
        blocks = gathered.at[owner, pl.ds(pl.multiple_of(4 * j, 4), 4)]
        return remote(blocks, blocks, send_sem.at[j], recv_sem.at[j], device)

    def to_core(j):
        return pass_on(j, view, core_s, core_r, other_core)

    def to_chip(j):
        return pass_on(j, view, mate_s, mate_r, other_chip)

    def onward(j):
        return pass_on(j, over, next_s, next_r, other_core)

    for copy in (to_core, to_chip, onward):
        later(0, NZ // 4, copy)

    def finish(j):
        pass_on(j, 2 * xh + 1 - core, core_s, core_r, other_core).wait_recv()
        pass_on(j, 2 * (1 - xh) + 1 - core, next_s, next_r, other_core).wait_recv()

        @pl.loop(0, 4)
        def _(n):
            i = 4 * j + n
            zt = lax.rem(z + NZ - jnp.where(i == 0, 0, far_first(i - 1)), NZ)
            for h in range(2):
                for t in range(4):
                    a, b = exchange_halves(gathered[2 * h, i, t], gathered[2 * h + 1, i, t])
                    turned[64 * h + 16 * t : 64 * h + 16 * t + 8, :] = a
                    turned[64 * h + 16 * t + 8 : 64 * h + 16 * t + 16, :] = b
            out[pl.ds(pl.multiple_of(BLOCK * zt, BLOCK), BLOCK), :] = turned[...].T

    @pl.loop(0, NZ // 4)
    def _(j):
        @pl.loop(jnp.where(j == 0, 1, 4 * j), 4 * j + 4)
        def _(i):
            y_sent(i).wait_recv()

        to_chip(j).start()
        to_core(j).start()

        @pl.when(j > 0)
        def _():
            pass_on(j - 1, over, mate_s, mate_r, other_chip).wait_recv()
            onward(j - 1).start()

    end = NZ // 4 - 1
    pass_on(end, over, mate_s, mate_r, other_chip).wait_recv()
    onward(end).start()

    @pl.loop(0, NZ // 4)
    def _(j):
        finish(j)

    for wait in leaving:
        wait()


def on_device(estimate, observed, long_taps, short_taps, brick_map, valid_rows):
    dma = pltpu.SemaphoreType.DMA
    vmem = pl.BlockSpec(memory_space=pltpu.VMEM)
    scratch = [
        ((ROWS, COLS), F32),
        ((ROWS, COLS), F32),
        ((VIEWS, 8, 128), F32),
        ((128, 128), F32),
        ((NZ, 4, 8, 128), F32),
        ((NZ, 4, 8, 128), F32),
        ((512, 128), F32),
        ((512, 128), F32),
        ((2048, 128), F32),
        ((VIEWS, 8, 64, 128), F32),
        ((ITERS, WIDE, TALL, 128), F32),
        ((WIDE, VIEWS * BLOCK, 128), F32),
        ((ITERS, VIEWS, WIDE, BLOCK, 128), F32),
        ((ITERS, VIEWS, OWN, TALL, 128), F32),
        ((VIEWS, OWN, BLOCK, 128), F32),
        ((512, 128), F32),
        ((8, 64, 128), F32),
        ((NZ, 4, 8, 128), F32),
        ((VIEWS, NZ, 4, 8, 128), F32),
        ((VIEWS * 8, 128), F32),
        *[((VIEWS, 256, 256), BF16)] * 2,
        *[((VIEWS * BLOCK, TALL), BF16)] * 4,
    ]
    semaphores = [
        (VIEWS,), (VIEWS,), (NZ,), (NZ,), (32,), (32,), (8,), (8,),
        (ITERS, 8), (ITERS, 8),
        (ITERS, VIEWS, 2), (ITERS, VIEWS, 2), (ITERS, VIEWS, 2), (ITERS, VIEWS, 2),
        (8,), (8,), (NZ,), (NZ,), (4,), (4,), (4,), (4,), (4,), (4,), (2,),
    ]
    refined = pl.pallas_call(
        kernel,
        out_shape=jax.ShapeDtypeStruct((ROWS, COLS), F32),
        in_specs=[pl.BlockSpec(memory_space=pl.ANY)] * 2 + [vmem] * 4,
        out_specs=vmem,
        scratch_shapes=[pltpu.VMEM(s, t) for s, t in scratch] + [dma(s) for s in semaphores],
        compiler_params=pltpu.CompilerParams(
            collective_id=0, has_side_effects=True, vmem_limit_bytes=56 * 2**20
        ),
    )(
        estimate.reshape(ROWS, COLS),
        observed.reshape(BRICKS * 16, COLS),
        long_taps,
        short_taps.reshape(2, 7),
        brick_map,
        valid_rows,
    )
    return refined.reshape(1, ROWS, COLS)


def solution(mesh):
    fine = Mesh(mesh.devices.reshape(2, 2, NZ, NY, 2), AXES)
    view, bricks = ("xh", "core"), ("z", "y", "xl")
    placed = (
        P(bricks, None, None),
        P(view, None, bricks, None),
        P(view, None),
        P(view, None, None),
        P(view, None),
        P(view, None),
    )
    return jax.shard_map(
        on_device, mesh=fine, in_specs=placed, out_specs=P(bricks, None, None), check_vma=False
    )
```

```python
import jax
import jax.numpy as jnp
from jax import lax
from jax.experimental import pallas as pl
from jax.experimental.pallas import tpu as pltpu
from jax.sharding import Mesh
from jax.sharding import PartitionSpec as P

F32, BF16 = jnp.float32, jnp.bfloat16
ITERS = 2
VIEWS, BRICKS, ROWS, COLS = 4, 128, 2048, 128
NZ, NY = 16, 4
BLOCK = 128
OWN = 4
WIDE = OWN + 6
HALO = 16
TALL = BLOCK + 2 * HALO
AXES = ("xh", "core", "z", "y", "xl")
MESH = pl.DeviceIdType.MESH


def split(x):
    head = x.astype(BF16)
    return head, (x - head.astype(F32)).astype(BF16)


def dot3(ah, al, bh, bl):
    def dot(a, b):
        return jnp.dot(a, b, preferred_element_type=F32)

    return dot(ah, bh) + (dot(al, bh) + dot(ah, bl))


def doubled(matrix):
    head, tail = split(matrix)
    return jnp.concatenate(
        [jnp.concatenate([head, tail], axis=1), jnp.concatenate([head, jnp.zeros_like(tail)], axis=1)], axis=0
    )


def product(x, twice):
    both = jnp.dot(jnp.concatenate(split(x), axis=1), twice, preferred_element_type=F32)
    return both[:, :128] + both[:, 128:]


def exchange_halves(a, b):
    axis = a.ndim - 2
    top = lax.broadcasted_iota(jnp.int32, a.shape, axis) < 4
    first = jnp.where(top, a, pltpu.roll(b, 4, axis))
    second = jnp.where(top, pltpu.roll(a, 4, axis), b)
    return first, second


def loop(n, body):
    def step(i, carry):
        body(i)
        return carry

    lax.fori_loop(0, n, step, 0)


def kernel(
    est_ref, obs_ref, long_ref, short_ref, map_ref, valid_ref, out,
    est, obs, long_taps, short_taps, brick_map, valid_rows, res, par, turned, s1, r1, s2, r2, obs_out, obs_in, ext, rows_done, spread, tall, corr,
    x2, r3, s4, gathered, tile_taps, ahead, back, tf_h, tf_l, tb_h, tb_l,
    par_s, par_r, z_s, z_r, obs_s, obs_r, p_s, p_r, e_s, e_r, uc_s, uc_r, ur_s, ur_r,
    q_s, q_r, y_s, y_r, core_s, core_r, mate_s, mate_r, next_s, next_r, in_s, out_s,
):
    xh, core, z, y, xl = (lax.axis_index(a) for a in AXES)
    x = 2 * xh + xl
    kk = 4 * xl + lax.rem(y + x, NY)
    k = 8 * xh + kk
    g = 2 * k + core
    view = 2 * xh + core
    slab = 2 * y + xl
    place = view * 8 + slab

    def at_kk(xh_, core_, kk_):
        xl_ = kk_ // 4
        return xh_, core_, z, lax.rem(lax.rem(kk_, 4) + 8 - 2 * xh_ - xl_, NY), xl_

    def slab_of(kk_):
        _, _, _, y_, xl_ = at_kk(xh, core, kk_)
        return 2 * y_ + xl_

    def at_g(g_, z_=None):
        k_ = g_ // 2
        xh_, core_, _, y_, xl_ = at_kk(k_ // 8, lax.rem(g_, 2), lax.rem(k_, 8))
        return xh_, core_, z if z_ is None else z_, y_, xl_

    def at_z(z_):
        return xh, core, z_, y, xl

    def at_place(place_):
        return place_ // 16, lax.rem(place_ // 8, 2), z, lax.rem(place_ // 2, 4), lax.rem(place_, 2)

    def at_view(view_):
        return view_ // 2, lax.rem(view_, 2), z, y, xl

    def g_of(place_):
        xh_, _, _, y_, xl_ = at_place(place_)
        x_ = 2 * xh_ + xl_
        return 2 * (4 * x_ + lax.rem(y_ + x_, NY)) + lax.rem(place_ // 8, 2)

    def remote(src, dst, send, recv, device):
        return pltpu.make_async_remote_copy(
            src_ref=src, dst_ref=dst, send_sem=send, recv_sem=recv, device_id=device, device_id_type=MESH
        )

    leaving = []

    def later(first, last, copy, local=False):
        def wait():
            @pl.loop(first, last)
            def _(i):
                copy(i).wait() if local else copy(i).wait_send()

        leaving.append(wait)

    left, right = lax.rem(g + 31, 32), lax.rem(g + 1, 32)
    above, below = lax.rem(z + NZ - 1, NZ), lax.rem(z + 1, NZ)

    pairs = (
        (est_ref, est), (obs_ref, obs), (long_ref, long_taps), (short_ref, short_taps), (map_ref, brick_map),
        (valid_ref, valid_rows),
    )
    loads = [
        pltpu.make_async_copy(a, b, in_s.at[i]) for i, (a, b) in enumerate(pairs)
    ]
    for load in loads:
        load.start()

    barrier = pltpu.get_barrier_semaphore()

    @pl.loop(1, NZ)
    def _(d):
        pl.semaphore_signal(barrier, inc=1, device_id=at_z(lax.rem(z + d, NZ)), device_id_type=MESH)

    @pl.loop(1, 32)
    def _(n):
        pl.semaphore_signal(barrier, inc=1, device_id=at_place(lax.rem(place + n, 32)), device_id_type=MESH)

    for g_ in (left, right):
        for z_ in (above, below):
            pl.semaphore_signal(barrier, inc=1, device_id=at_g(g_, z_), device_id_type=MESH)

    for load in loads[2:]:
        load.wait()

    par[view] = jnp.zeros((8, 128), F32)
    par[view, 0:1, :] = brick_map[...].astype(F32)
    par[view, 1:2, :] = valid_rows[...].astype(F32)
    par[view, 2:3, 0:31] = long_taps[...]
    par[view, 3:5, 0:7] = short_taps[...]

    loads[0].wait()

    def piece_for(zt):
        block = est[pl.ds(pl.multiple_of(BLOCK * zt, BLOCK), BLOCK), :]
        turned[...] = block.T
        half = turned[pl.ds(pl.multiple_of(64 * xh, 64), 64), :].reshape(4, 2, 8, 128)
        first, second = exchange_halves(half[:, 0], half[:, 1])
        return jnp.where(core == 0, first, second)

    def z_copy(d, source, device):
        return remote(s1.at[d], r1.at[source], z_s.at[d], z_r.at[d], device)

    def far_first(i):
        return 8 + ((i + 1) // 2) * (1 - 2 * lax.rem(i, 2))

    @pl.loop(1, NZ)
    def _(d):
        s1[d] = piece_for(lax.rem(z + d, NZ))

    r1[z] = piece_for(z)

    loads[1].wait()

    @pl.loop(0, 16)
    def _(r):
        obs_out[pl.ds(r, 128, stride=16), :] = obs[pl.ds(r, 128, stride=16), :].T

    pl.semaphore_wait(barrier, NZ - 1 + 31 + 4)

    def par_copy(m, source, device):
        return remote(par.at[source], par.at[source], par_s.at[m], par_r.at[m], device)

    for m in range(1, VIEWS):
        par_copy(m, view, at_view(lax.rem(view + m, VIEWS))).start()
    later(1, VIEWS, lambda m: par_copy(m, view, at_view(lax.rem(view + m, VIEWS))))

    @pl.loop(0, NZ - 1)
    def _(i):
        d = far_first(i)
        z_copy(d, z, at_z(lax.rem(z + d, NZ))).start()

    later(1, NZ, lambda d: z_copy(d, z, at_z(lax.rem(z + d, NZ))))

    def obs_copy(n, g_, view_, slab_, device):
        src = obs_out.at[pl.ds(pl.multiple_of(64 * g_, 64), 64)]
        return remote(src, obs_in.at[view_, slab_], obs_s.at[n], obs_r.at[n], device)

    @pl.loop(1, 32)
    def _(n):
        to = lax.rem(place + n, 32)
        obs_copy(n, g_of(to), view, slab, at_place(to)).start()

    def obs_sent(n):
        to = lax.rem(place + n, 32)
        return obs_copy(n, g_of(to), view, slab, at_place(to))

    later(1, 32, obs_sent)
    obs_in[view, slab] = obs_out[pl.ds(pl.multiple_of(64 * g, 64), 64), :]

    for m in range(1, VIEWS):
        par_copy(m, lax.rem(view + VIEWS - m, VIEWS), at_view(lax.rem(view + m, VIEWS))).wait_recv()
    lane = lax.broadcasted_iota(jnp.int32, (1, 128), 1)
    order = lax.broadcasted_iota(jnp.int32, (128, 128), 0)
    brick = (lax.rem(order, 16) * 8 + order // 16).astype(F32)
    tall_lane = lax.broadcasted_iota(jnp.int32, (BLOCK, TALL), 1)
    inside = jnp.logical_and(
        jnp.logical_or(tall_lane >= HALO, z > 0), jnp.logical_or(tall_lane < HALO + BLOCK, z < NZ - 1)
    )
    for v in range(VIEWS):
        bricks, long_row, plane, column = (par[v, i : i + 1, :] for i in (0, 2, 3, 4))
        long_row, plane, column = (t / jnp.sum(t, axis=1, keepdims=True) for t in (long_row, plane, column))
        matrix = jnp.zeros((128, 128), F32)
        for t in range(7):
            near = pltpu.roll(bricks, (3 - t) % 128, 1)
            near = jnp.where(jnp.logical_and(lane + (t - 3) >= 0, lane + (t - 3) < BRICKS), near, -1.0)
            matrix += jnp.where(brick == near, plane[:, t : t + 1], 0.0)
            tile_taps[8 * v + t : 8 * v + t + 1, :] = jnp.broadcast_to(column[:, t : t + 1], (1, 128))
        ahead[v], back[v] = doubled(matrix), doubled(matrix.T)
        padded = jnp.concatenate([long_row, jnp.zeros((1, 128), F32)], axis=1)
        wide = jnp.broadcast_to(padded, (BLOCK, 256))
        toeplitz = pltpu.roll(wide, 1, 1, stride=1, stride_axis=0)[:, :TALL]
        tf_h[pl.ds(BLOCK * v, BLOCK), :], tf_l[pl.ds(BLOCK * v, BLOCK), :] = split(
            jnp.where(inside, toeplitz, 0.0)
        )
        high = jnp.broadcast_to(padded, (256, 256))
        flipped = pltpu.roll(high, 225, 1, stride=1, stride_axis=0)[:, :128].T[:, :TALL]
        tb_h[pl.ds(BLOCK * v, BLOCK), :], tb_l[pl.ds(BLOCK * v, BLOCK), :] = split(
            jnp.where(inside, flipped, 0.0)
        )

    @pl.loop(0, NZ - 1)
    def _(i):
        d = far_first(i)
        z_copy(d, lax.rem(z + NZ - d, NZ), at_z(lax.rem(z + d, NZ))).wait_recv()

    @pl.loop(0, 8)
    def _(m):
        first, second = exchange_halves(r1[2 * m], r1[2 * m + 1])
        for i in range(4):
            s2[pl.ds(pl.multiple_of(64 * (2 * i) + 8 * m, 8), 8), :] = first[i]
            s2[pl.ds(pl.multiple_of(64 * (2 * i + 1) + 8 * m, 8), 8), :] = second[i]

    def p_copy(n, kt, source):
        src = s2.at[pl.ds(pl.multiple_of(64 * kt, 64), 64)]
        dst = r2.at[pl.ds(pl.multiple_of(64 * slab_of(source), 64), 64)]
        return remote(src, dst, p_s.at[n], p_r.at[n], at_kk(xh, core, kt))

    @pl.loop(1, 8)
    def _(n):
        p_copy(n, lax.rem(kk + n, 8), kk).start()

    later(1, 8, lambda n: p_copy(n, lax.rem(kk + n, 8), kk))
    mine = pl.ds(pl.multiple_of(64 * slab, 64), 64)
    r2[mine, :] = s2[pl.ds(pl.multiple_of(64 * kk, 64), 64), :]

    @pl.loop(1, 8)
    def _(n):
        p_copy(n, lax.rem(kk + n, 8), lax.rem(kk + 8 - n, 8)).wait_recv()

    for c in range(OWN):
        ext[0, 3 + c, HALO : HALO + BLOCK, :] = r2[pl.ds(c, 128, stride=4), :].T

    def observed_arrives():
        @pl.loop(1, 32)
        def _(n):
            source = lax.rem(place + 32 - n, 32)
            to = lax.rem(place + n, 32)
            obs_copy(n, g_of(to), source // 8, lax.rem(source, 8), at_place(to)).wait_recv()

    middle = pl.ds(HALO, BLOCK)

    first, last = pl.ds(HALO, HALO), pl.ds(BLOCK, HALO)
    before, after = pl.ds(0, HALO), pl.ds(HALO + BLOCK, HALO)

    def ext_copy(it, i, columns, rows, to_columns, to_rows, device):
        return remote(
            ext.at[it, columns, rows], ext.at[it, to_columns, to_rows], e_s.at[it, i], e_r.at[it, i], device
        )

    def ext_sides(it):
        return (
            ext_copy(it, 0, pl.ds(3, 3), middle, pl.ds(7, 3), middle, at_g(left)),
            ext_copy(it, 1, pl.ds(4, 3), middle, pl.ds(0, 3), middle, at_g(right)),
            ext_copy(it, 2, pl.ds(3, 3), first, pl.ds(7, 3), after, at_g(left, above)),
            ext_copy(it, 3, pl.ds(3, 3), last, pl.ds(7, 3), before, at_g(left, below)),
            ext_copy(it, 4, pl.ds(4, 3), first, pl.ds(0, 3), after, at_g(right, above)),
            ext_copy(it, 5, pl.ds(4, 3), last, pl.ds(0, 3), before, at_g(right, below)),
        )

    def ext_rows(it):
        own = pl.ds(3, OWN)
        return (
            ext_copy(it, 6, own, first, own, after, at_z(above)),
            ext_copy(it, 7, own, last, own, before, at_z(below)),
        )

    def spread_columns(it, v):
        return (
            remote(spread.at[it, v, 3:6], spread.at[it, v, 7:10], uc_s.at[it, v, 0], uc_r.at[it, v, 0], at_g(left)),
            remote(spread.at[it, v, 4:7], spread.at[it, v, 0:3], uc_s.at[it, v, 1], uc_r.at[it, v, 1], at_g(right)),
        )

    def tall_rows(it, v):
        return (
            remote(tall.at[it, v, :, first], tall.at[it, v, :, after], ur_s.at[it, v, 0], ur_r.at[it, v, 0], at_z(above)),
            remote(tall.at[it, v, :, last], tall.at[it, v, :, before], ur_s.at[it, v, 1], ur_r.at[it, v, 1], at_z(below)),
        )

    def column_inside(i):
        at = OWN * g + i - 3
        return jnp.logical_and(at >= 0, at < COLS)

    row_ids = (BLOCK * z + lax.broadcasted_iota(jnp.int32, (BLOCK, 128), 0)).astype(F32)

    def send(copies):
        for copy in copies:
            copy.start()

    def arrive(copies):
        for copy in copies:
            copy.wait_recv()

    def blur_rows(it, i, j):
        pair = jnp.concatenate([jnp.where(column_inside(n), ext[it, n], 0.0) for n in (i, j)], axis=1)
        done = dot3(tf_h[...], tf_l[...], *split(pair))
        rows_done[i], rows_done[j] = done[:, :128], done[:, 128:]

    def back_projected(v):
        part = pl.ds(pl.multiple_of(BLOCK * v, BLOCK), BLOCK)
        taps = [tile_taps[pl.ds(8 * v + t, 1), :] for t in range(7)]
        blurred = jnp.concatenate(
            [sum(taps[t] * rows_done[c + t, part, :] for t in range(7)) for c in range(OWN)], axis=0
        )
        blurred = product(blurred, ahead[v])
        ratios = []
        for c in range(OWN):
            seen = obs_in[v, :, 16 * c : 16 * c + 16, :].reshape(BLOCK, 128)
            ratio = seen / blurred[BLOCK * c : BLOCK * c + BLOCK]
            ratios.append(jnp.where(row_ids < par[v, 1:2, :], ratio, 1.0))
        return product(jnp.concatenate(ratios, axis=0), back[v]).reshape(OWN, BLOCK, 128)

    def columns_back(it, v, c):
        total = jnp.zeros((BLOCK, 128), F32)
        for t in range(7):
            tap = jnp.where(column_inside(c + t), tile_taps[pl.ds(8 * v + 6 - t, 1), :], 0.0)
            total += tap * spread[it, v, c + t]
        return total

    def rows_back(it, v):
        part = pl.ds(pl.multiple_of(BLOCK * v, BLOCK), BLOCK)
        beside = jnp.concatenate([tall[it, v, c] for c in range(OWN)], axis=1)
        done = dot3(tb_h[part, :], tb_l[part, :], *split(beside))
        return [done[:, 128 * c : 128 * c + 128] for c in range(OWN)]

    for it in range(ITERS):
        send(ext_sides(it))
        send(ext_rows(it))
        leaving.extend(copy.wait_send for copy in (*ext_sides(it), *ext_rows(it)))
        arrive(ext_rows(it))

        @pl.loop(0, 2)
        def _(i):
            blur_rows(it, 3 + 2 * i, 4 + 2 * i)

        arrive(ext_sides(it))

        @pl.loop(0, 3)
        def _(i):
            blur_rows(it, 2 * i + 4 * (i // 2), 1 + 6 * ((i + 1) // 2) + 2 * (i // 2))

        if it == 0:
            observed_arrives()

        @pl.loop(0, 2)
        def _(v):
            spread[it, v, 3 : 3 + OWN] = back_projected(v)
            send(spread_columns(it, v))

        @pl.loop(2, VIEWS)
        def _(v):
            tall[it, v, :, HALO : HALO + BLOCK, :] = back_projected(v)
            send(tall_rows(it, v))

        @pl.loop(2, VIEWS)
        def _(v):
            arrive(tall_rows(it, v))

            for c, done in enumerate(rows_back(it, v)):
                spread[it, v, 3 + c] = done
            send(spread_columns(it, v))

        @pl.loop(0, 2)
        def _(v):
            arrive(spread_columns(it, v))

            @pl.loop(0, OWN)
            def _(c):
                tall[it, v, c, HALO : HALO + BLOCK, :] = columns_back(it, v, c)

            send(tall_rows(it, v))

        @pl.loop(0, 2)
        def _(v):
            arrive(tall_rows(it, v))

            for c, done in enumerate(rows_back(it, v)):
                corr[v, c] = done

        @pl.loop(2, VIEWS)
        def _(v):
            arrive(spread_columns(it, v))

            @pl.loop(0, OWN)
            def _(c):
                corr[v, c] = columns_back(it, v, c)

        for i in range(2):
            later(0, VIEWS, lambda v, i=i, it=it: spread_columns(it, v)[i])
            later(0, VIEWS, lambda v, i=i, it=it: tall_rows(it, v)[i])

        for c in range(OWN):
            log_total = jnp.log(corr[0, c] * corr[1, c]) + jnp.log(corr[2, c] * corr[3, c])
            current = ext[it, 3 + c, HALO : HALO + BLOCK, :] * jnp.exp(log_total)
            if it < ITERS - 1:
                ext[it + 1, 3 + c, HALO : HALO + BLOCK, :] = current
            else:
                x2[pl.ds(c, 128, stride=4), :] = current.T

    def q_copy(n, kt, source):
        src = x2.at[pl.ds(pl.multiple_of(64 * slab_of(kt), 64), 64)]
        return remote(src, r3.at[source], q_s.at[n], q_r.at[n], at_kk(xh, core, kt))

    @pl.loop(1, 8)
    def _(n):
        q_copy(n, lax.rem(kk + n, 8), kk).start()

    later(1, 8, lambda n: q_copy(n, lax.rem(kk + n, 8), kk))
    r3[kk] = x2[mine, :]

    @pl.loop(1, 8)
    def _(n):
        q_copy(n, lax.rem(kk + n, 8), lax.rem(kk + 8 - n, 8)).wait_recv()

    @pl.loop(0, 8)
    def _(m):
        part = pl.ds(pl.multiple_of(8 * m, 8), 8)
        for i in range(4):
            first, second = exchange_halves(r3[2 * i, part, :], r3[2 * i + 1, part, :])
            s4[2 * m, i] = first
            s4[2 * m + 1, i] = second

    def y_copy(i, device):
        d = far_first(i - 1)
        return remote(s4.at[lax.rem(z + d, NZ)], gathered.at[view, i], y_s.at[i], y_r.at[i], device)

    def y_sent(i):
        return y_copy(i, at_z(lax.rem(z + far_first(i - 1), NZ)))

    @pl.loop(1, NZ)
    def _(i):
        y_sent(i).start()

    later(1, NZ, y_sent)
    gathered[view, 0] = s4[z]

    other_core, other_chip = (xh, 1 - core, z, y, xl), (1 - xh, core, z, y, xl)
    over = 2 * (1 - xh) + core

    def pass_on(j, owner, send_sem, recv_sem, device):
        blocks = gathered.at[owner, pl.ds(pl.multiple_of(4 * j, 4), 4)]
        return remote(blocks, blocks, send_sem.at[j], recv_sem.at[j], device)

    def to_core(j):
        return pass_on(j, view, core_s, core_r, other_core)

    def to_chip(j):
        return pass_on(j, view, mate_s, mate_r, other_chip)

    def onward(j):
        return pass_on(j, over, next_s, next_r, other_core)

    def from_chip(j):
        return pass_on(j, over, mate_s, mate_r, other_chip)

    straight = pass_on(NZ // 4 - 1, view, next_s, next_r, (1 - xh, 1 - core, z, y, xl))
    later(0, NZ // 4, to_core)
    later(0, NZ // 4, to_chip)
    later(0, NZ // 4 - 1, onward)
    leaving.append(straight.wait_send)

    def block_of(i):
        return lax.rem(z + NZ - jnp.where(i == 0, 0, far_first(i - 1)), NZ)

    def out_copy(i):
        rows = pl.ds(pl.multiple_of(BLOCK * block_of(i), BLOCK), BLOCK)
        return pltpu.make_async_copy(res.at[rows], out.at[rows], out_s.at[i])

    def finish(j):
        pass_on(j, 2 * xh + 1 - core, core_s, core_r, other_core).wait_recv()
        pass_on(j, 2 * (1 - xh) + 1 - core, next_s, next_r, other_core).wait_recv()

        @pl.loop(0, 4)
        def _(n):
            i = 4 * j + n
            zt = block_of(i)
            for h in range(2):
                for t in range(4):
                    a, b = exchange_halves(gathered[2 * h, i, t], gathered[2 * h + 1, i, t])
                    turned[64 * h + 16 * t : 64 * h + 16 * t + 8, :] = a
                    turned[64 * h + 16 * t + 8 : 64 * h + 16 * t + 16, :] = b
            rows = pl.ds(pl.multiple_of(BLOCK * zt, BLOCK), BLOCK)
            res[rows, :] = turned[...].T
            out_copy(i).start()

    end = NZ // 4 - 1
    for j in range(NZ // 4):

        @pl.loop(max(1, 4 * j), 4 * j + 4)
        def _(i):
            y_sent(i).wait_recv()

        to_chip(j).start()
        if j == end:
            straight.start()
        to_core(j).start()
        if j > 0:
            from_chip(j - 1).wait_recv()
            onward(j - 1).start()
        if j > 1:
            finish(j - 2)
    finish(end - 1)
    from_chip(end).wait_recv()
    finish(end)

    later(0, NZ, out_copy, local=True)

    for wait in leaving:
        wait()


def on_device(estimate, observed, long_taps, short_taps, brick_map, valid_rows):
    dma = pltpu.SemaphoreType.DMA
    there = pl.BlockSpec(memory_space=pl.ANY)
    scratch = [
        ((ROWS, COLS), F32),
        ((ROWS, COLS), F32),
        ((1, 31), F32),
        ((2, 7), F32),
        ((1, 128), jnp.int32),
        ((1, 128), jnp.int32),
        ((ROWS, COLS), F32),
        ((VIEWS, 8, 128), F32),
        ((128, 128), F32),
        ((NZ, 4, 8, 128), F32),
        ((NZ, 4, 8, 128), F32),
        ((512, 128), F32),
        ((512, 128), F32),
        ((2048, 128), F32),
        ((VIEWS, 8, 64, 128), F32),
        ((ITERS, WIDE, TALL, 128), F32),
        ((WIDE, VIEWS * BLOCK, 128), F32),
        ((ITERS, VIEWS, WIDE, BLOCK, 128), F32),
        ((ITERS, VIEWS, OWN, TALL, 128), F32),
        ((VIEWS, OWN, BLOCK, 128), F32),
        ((512, 128), F32),
        ((8, 64, 128), F32),
        ((NZ, 4, 8, 128), F32),
        ((VIEWS, NZ, 4, 8, 128), F32),
        ((VIEWS * 8, 128), F32),
        *[((VIEWS, 256, 256), BF16)] * 2,
        *[((VIEWS * BLOCK, TALL), BF16)] * 4,
    ]
    semaphores = [
        (VIEWS,), (VIEWS,), (NZ,), (NZ,), (32,), (32,), (8,), (8,),
        (ITERS, 8), (ITERS, 8),
        (ITERS, VIEWS, 2), (ITERS, VIEWS, 2), (ITERS, VIEWS, 2), (ITERS, VIEWS, 2),
        (8,), (8,), (NZ,), (NZ,), (4,), (4,), (4,), (4,), (4,), (4,), (6,), (NZ,),
    ]
    refined = pl.pallas_call(
        kernel,
        out_shape=jax.ShapeDtypeStruct((ROWS, COLS), F32),
        in_specs=[there] * 6,
        out_specs=there,
        scratch_shapes=[pltpu.VMEM(s, t) for s, t in scratch] + [dma(s) for s in semaphores],
        compiler_params=pltpu.CompilerParams(
            collective_id=0, has_side_effects=True, vmem_limit_bytes=56 * 2**20
        ),
    )(
        estimate.reshape(ROWS, COLS),
        observed.reshape(BRICKS * 16, COLS),
        long_taps,
        short_taps.reshape(2, 7),
        brick_map,
        valid_rows,
    )
    return refined.reshape(1, ROWS, COLS)


def solution(mesh):
    fine = Mesh(mesh.devices.reshape(2, 2, NZ, NY, 2), AXES)
    view, bricks = ("xh", "core"), ("z", "y", "xl")
    placed = (
        P(bricks, None, None),
        P(view, None, bricks, None),
        P(view, None),
        P(view, None, None),
        P(view, None),
        P(view, None),
    )
    return jax.shard_map(
        on_device, mesh=fine, in_specs=placed, out_specs=P(bricks, None, None), check_vma=False
    )
```
